32 devices in a mesh: gx: 8 (over y, x, core), gy: 4 (over z).
Axes of the slice: x: 2, y: 2, z: 4, core: 2. Of those that a mesh axis runs over, the one named last changes fastest.
Arguments:
- fields: float32 [4, 4, 320, 10240], P(None, None, 'gy', 'gx'), may hold values from -6 to 6
- owner: int32 [2048, 1], P(('gx', 'gy')), may hold values from 0 to 31; in each aligned block of 64 rows (0 to 63, 64 to 127, ...) at most 4 rows name the same one
Outputs:
- received: float32 [4096, 640], P(('gx', 'gy'))
The draws below stay inside these ranges and needn't reach their ends.
Inputs may be any that keep to these rules, and one draw needn't show every extreme that they name: Among the blocks of one device, no owner is named more than 4 times, a bound that some block reaches.
All inputs are finite; a program needn't handle non-finite values.
Results may differ from the reference program's by a relative error of at most 0.0001.
Values sent between devices are 32-bit elements; how exact they have to be, the bound alone decides.
No kernel may reach another device: no remote copies, remote signals or barrier semaphores. Data moves between devices by JAX's collectives and lax.ppermute only.
A program may use at most 256 MiB of HBM per device.

```python
import math
import jax
import jax.numpy as jnp
import numpy as np
from jax import lax

LEV = 4
BLK = 4
NX = 10240
NY = 320
NBX = 32
NBY = 2
NB_DEV = 64
NBLOCKS = 2048
PAIRCAP = 4
PAY = 640
SLOTS = 4096
N_GX = 8
N_GY = 4
DEVICES = 32


def steps_of(key, shape, pieces, least, largest):
    loudness, own = 1.0, jax.random.fold_in(key, 6)
    for dim, shards_of in pieces:
        heights = jnp.exp(jax.random.uniform(jax.random.fold_in(own, dim), (shards_of,), jnp.float32, least / len(pieces), largest / len(pieces)))
        loudness = loudness * jnp.repeat(heights, shape[dim] // shards_of).reshape([-1 if axis == dim else 1 for axis in range(len(shape))])
    return loudness


def deal_out(key, own, number, rows, count, top, limit, skew):
    sequence = jax.random.permutation(key, count)
    heavy_load, ordinary = load_shares(count, rows * top, limit, skew, True), load_shares(count, rows * top, limit, skew, False)
    places = jnp.arange(count)

    def named(lengths, turn):
        used = int((lengths > 0).sum())
        fixed = max(1, used // 4)
        moved = fixed + (places - fixed + turn * (used - fixed)) % max(1, count - fixed)
        return jnp.zeros((count,), jnp.int32).at[sequence[jnp.where(places < fixed, places, moved)]].set(jnp.asarray(lengths, jnp.int32))

    lengths = jnp.where(number % 4 == 0, named(heavy_load, number // 4), named(ordinary, number - number // 4 - 1))
    mixed = jax.random.permutation(jax.random.fold_in(own, 3), count)
    source_of, sink = mixed[0:count // 2 * 2:2], mixed[1:count // 2 * 2:2]
    room = jnp.minimum(lengths[source_of] - 1, limit - lengths[sink]) // 2
    room = jnp.where((source_of == sequence[0]) | (sink == sequence[0]) | (lengths[sink] == 0), 0, jnp.maximum(room, 0))
    moved = jax.random.randint(jax.random.fold_in(own, 4), (count // 2,), 0, 1 << 20) % (room + 1)
    lengths = lengths.at[source_of].add(-moved).at[sink].add(moved)
    items = jnp.searchsorted(jnp.cumsum(lengths), jnp.arange(rows * top), side="right").astype(jnp.int32)
    table = items.reshape(top, rows).T
    table = table[jax.random.permutation(jax.random.fold_in(own, 1), rows)]
    turn = jax.random.randint(jax.random.fold_in(own, 2), (rows, 1), 0, top)
    return jnp.take_along_axis(table, (jnp.arange(top)[None, :] + turn) % top, axis=1)


def load_shares(amount, total, reach, slope, full):
    portions = [(1 << 20) // math.isqrt(standing ** slope) + 1 for standing in range(1, amount + 1)]
    largest = reach if full else min(reach, max(-(-total // amount), total * portions[0] // sum(portions)))
    least = 1 if total - largest >= amount - 1 else 0
    holding, spare = [largest] + [least] * (amount - 1), total - largest - least * (amount - 1)
    while spare > 0:
        candidates = [i for i in range(1, amount) if holding[i] < largest] or [i for i in range(1, amount) if holding[i] < reach]
        pool, budget = sum([portions[i] for i in candidates]), spare
        for i in candidates:
            extra = min(reach - holding[i], max(1, budget * portions[i] // pool), spare)
            holding[i] = holding[i] + extra
            spare = spare - extra
    return np.array(holding)


def centred(rng, dims, deviation, most, pieces=(), held_as=jnp.bfloat16):
    factor_of = steps_of(rng, dims, pieces, -0.22, 0.18) if pieces else 1.0
    entries = jax.random.normal(rng, dims, jnp.float32) * deviation * factor_of
    return jnp.minimum(jnp.maximum(entries, -most), most).astype(held_as)


def setup_inputs(seed: int = 0) -> dict:
    arg_keys = jax.random.split(jax.random.key(seed), 3)
    fields = centred(arg_keys[0], (4, LEV, NY, NX), 1.0, 6.0, ((2, 4), (3, 8)), jnp.float32)
    owner_keys = jax.random.split(jax.random.fold_in(arg_keys[1], 1), NBLOCKS // NB_DEV)
    owner_turns = jax.random.permutation(jax.random.fold_in(arg_keys[1], 3), NBLOCKS // NB_DEV)
    owner = jax.vmap(lambda own, number: deal_out(jax.random.fold_in(arg_keys[1], 2), own, number, NB_DEV, DEVICES, 1, PAIRCAP, 2))(owner_keys, owner_turns).reshape((NBLOCKS, 1))
    return {"fields": fields, "owner": owner}


SIGMA_CELLS = 2.8867513
PRODUCT_PAIRS = ((0, 0), (0, 1), (0, 2), (0, 3), (1, 1), (1, 2), (1, 3), (2, 2), (2, 3), (3, 3))


def gauss_taps():
    spread = jnp.arange(21, dtype=jnp.float32) - 10.0
    values = jnp.exp(-spread * spread / (2.0 * SIGMA_CELLS * SIGMA_CELLS))
    return values / jnp.sum(values)


def filter_last(field, weights):
    length = field.shape[-1]
    coarse_len = length // 10
    padded = jnp.concatenate([field[..., length - 5:], field, field[..., :15]], axis=-1)
    groups = padded.reshape(field.shape[:-1] + (coarse_len + 2, 10))
    lead_part = jnp.sum(groups[..., :coarse_len, :] * weights[:10], axis=-1)
    next_part = jnp.sum(groups[..., 1:coarse_len + 1, :] * weights[10:20], axis=-1)
    tail_part = groups[..., 2:coarse_len + 2, 0] * weights[20]
    return lead_part + next_part + tail_part


def filter_plane(field, weights):
    along_east = filter_last(field, weights)
    return jnp.swapaxes(filter_last(jnp.swapaxes(along_east, -1, -2), weights), -1, -2)


def reference(fields, owner):
    weights = gauss_taps()

    def one_level(level_index):
        level_field = lax.dynamic_index_in_dim(fields, level_index, 1, keepdims=False)
        components = [level_field[c] for c in range(4)]
        coarse_means = [filter_plane(c, weights) for c in components]
        pair_terms = []
        for first_idx, second_idx in PRODUCT_PAIRS:
            product = filter_plane(components[first_idx] * components[second_idx], weights)
            pair_terms.append(product - coarse_means[first_idx] * coarse_means[second_idx])
        return jnp.stack(pair_terms)

    stresses = lax.map(one_level, jnp.arange(LEV, dtype=jnp.int32))
    stresses = jnp.moveaxis(stresses, 0, 1)
    blocks = stresses.reshape(10, LEV, N_GY, NBY, BLK, N_GX, NBX, BLK)
    blocks = jnp.transpose(blocks, (5, 2, 3, 6, 0, 1, 4, 7)).reshape(NBLOCKS, PAY)
    destination = owner[:, 0].reshape(DEVICES, NB_DEV)
    onehot = (destination[:, :, None] == jnp.arange(DEVICES, dtype=jnp.int32)[None, None, :]).astype(jnp.int32)
    before = jnp.cumsum(onehot, axis=1) - onehot
    place_rank = jnp.sum(before * onehot, axis=2)
    source = jnp.arange(DEVICES, dtype=jnp.int32)[:, None]
    target = destination * (DEVICES * PAIRCAP) + source * PAIRCAP + place_rank
    received = jnp.zeros((SLOTS, PAY), jnp.float32).at[target.reshape(-1)].set(blocks)
    return received
```

```python
import functools

import jax
import jax.numpy as jnp
import numpy as np
from jax import lax
from jax.experimental import pallas as pl
from jax.experimental.pallas import tpu as pltpu
from jax.sharding import PartitionSpec as P

BLK = 4
RATIO = 10
LANES = 128
HIGHEST = lax.Precision.HIGHEST
SIGMA_CELLS = 2.8867513
PRODUCT_PAIRS = ((0, 0), (0, 1), (0, 2), (0, 3), (1, 1), (1, 2), (1, 3), (2, 2), (2, 3), (3, 3))
COMPONENTS = 4
TERMS = COMPONENTS + len(PRODUCT_PAIRS)
LEVELS = 4
ROWS = 8
VMEM_BYTES = 24 * 1024 * 1024


def gauss_taps():
    spread = np.arange(21, dtype=np.float64) - 10.0
    values = np.exp(-spread * spread / (2.0 * SIGMA_CELLS * SIGMA_CELLS))
    return (values / values.sum()).astype(np.float32)


TAPS = gauss_taps()
G = [float(v) for v in TAPS]


def east_weights(columns):
    fine = np.arange(columns)[:, None]
    coarse = np.arange(columns // RATIO)[None, :]
    tap = fine - RATIO * coarse + 5
    inside = (tap >= 0) & (tap <= 20)
    return np.where(inside, TAPS[np.clip(tap, 0, 20)], np.float32(0))


def beyond_weights():
    weights = np.zeros((2, 8, LANES), np.float32)
    weights[0, 0, :6] = TAPS[15:21]
    weights[1, 0, LANES - 5 :] = TAPS[0:5]
    return weights


def edge_places():
    places = np.zeros((16, LANES), np.float32)
    places[0, LANES - 1] = 1.0
    places[8, 0] = 1.0
    return places


def north_tile(field, level, store):
    def loads(p):
        return [field[c * LEVELS + level, pl.ds(p, ROWS, stride=RATIO), :] for c in range(COMPONENTS)]

    def weighed(values, weight, sums):
        scaled = [v * weight for v in values]
        terms = scaled + [scaled[a] * values[b] for a, b in PRODUCT_PAIRS]
        return terms if sums is None else [s + t for s, t in zip(sums, terms)]

    own = below = above = None
    for p in range(RATIO):
        values = loads(p)
        own = weighed(values, G[p + 5], own)
        if p <= 5:
            below = weighed(values, G[p + 15], below)
        if p >= 5:
            above = weighed(values, G[p - 5], above)
    row = lax.broadcasted_iota(jnp.int32, (ROWS, LANES), 0)
    for q in range(TERMS):
        from_next = jnp.where(row < ROWS - 1, pltpu.roll(below[q], ROWS - 1, 0), 0.0)
        from_last = jnp.where(row > 0, pltpu.roll(above[q], 1, 0), 0.0)
        store(q * LEVELS + level, own[q] + from_next + from_last, below[q][0:1, :], above[q][ROWS - 1 : ROWS, :])


def store_in(inner, edge, lead):
    def store(place, inside, before, after):
        inner[lead, pl.ds(place * ROWS, ROWS), :] = inside
        edge[lead, pl.ds(place, 1), :] = before
        edge[lead, pl.ds(TERMS * LEVELS + place, 1), :] = after

    return store


def side_kernel(fields, weights, inner, edge, message, tile, sems):
    last = fields.shape[-1] - LANES
    copies = [
        pltpu.make_async_copy(fields.at[:, :, pl.ds(start, LANES)], tile.at[side], sems.at[side])
        for side, start in enumerate((0, last))
    ]
    for copy in copies:
        copy.start()
    for side, copy in enumerate(copies):
        copy.wait()
        for level in range(LEVELS):
            north_tile(tile.at[side], level, store_in(inner, edge, side))
        sums = jnp.concatenate([inner[side], edge[side]], axis=0)
        message[side] = lax.dot_general(
            weights[side], sums, (((1,), (1,)), ((), ())), precision=HIGHEST, preferred_element_type=jnp.float32
        )


def inner_kernel(fields, inner, edge, tile, sems):
    count = inner.shape[0]

    def copy(t):
        return pltpu.make_async_copy(
            fields.at[:, :, pl.ds(pl.multiple_of((t + 1) * LANES, LANES), LANES)], tile.at[t], sems.at[t]
        )

    for t in range(count):
        copy(t).start()

    def step(t, carry):
        copy(t).wait()
        for level in range(LEVELS):
            north_tile(tile.at[t], level, store_in(inner, edge, t))
        return carry

    lax.fori_loop(0, count, step, 0)


def east_sums(sides, inner, weights):
    count = inner.shape[0]
    tiles = [sides[0]] + [inner[t] for t in range(count)] + [sides[1]]
    total = None
    for t in range(0, count + 2, 2):
        pair = jnp.concatenate(tiles[t : t + 2], axis=1)
        part = jnp.dot(
            pair, weights[t * LANES : (t + 2) * LANES, :], precision=HIGHEST, preferred_element_type=jnp.float32
        )
        total = part if total is None else total + part
    return total


def from_sides(east, west, places):
    both = jnp.concatenate([east, west], axis=0)
    return lax.dot_general(
        both, places[...], (((0,), (0,)), ((), ())), precision=HIGHEST, preferred_element_type=jnp.float32
    )


def edge_kernel(sides, edge, weights, places, east, west, before, after):
    start = TERMS * LEVELS * ROWS
    total = east_sums(sides, edge, weights) + from_sides(east[:, start:], west[:, start:], places)
    half = TERMS * LEVELS
    before[...] = total[:half]
    after[...] = total[half:]


def coarse_kernel(sides, inner, weights, places, east, west, coarse):
    stop = TERMS * LEVELS * ROWS
    coarse[...] = east_sums(sides, inner, weights) + from_sides(east[:, :stop], west[:, :stop], places)


def send_kernel(cap, coarse, north, south, owner, outgoing, filtered, spread):
    filtered[...] = coarse[...]
    half = TERMS * LEVELS
    filtered[pl.ds(0, half, stride=ROWS), :] += south[...]
    filtered[pl.ds(ROWS - 1, half, stride=ROWS), :] += north[...]
    slab = LEVELS * ROWS
    means = [filtered[c * slab : (c + 1) * slab, :] for c in range(COMPONENTS)]
    lane = lax.broadcasted_iota(jnp.int32, (slab, LANES), 1) % BLK
    for k, (a, b) in enumerate(PRODUCT_PAIRS):
        q = COMPONENTS + k
        stress = filtered[q * slab : (q + 1) * slab, :] - means[a] * means[b]
        for c in range(BLK):
            spread[pl.ds(k * slab * BLK + c, slab, stride=BLK), :] = jnp.where(lane == c, stress, 0.0)
    slots = outgoing.shape[0] * outgoing.shape[1]
    blocks = owner.shape[0]
    across = LANES // BLK
    index = lax.broadcasted_iota(jnp.int32, (blocks, LANES), 0)
    named = jnp.broadcast_to(owner[...], (blocks, LANES))
    slot_row = lax.broadcasted_iota(jnp.int32, (slots, LANES), 0)
    stresses = spread[...].reshape(len(PRODUCT_PAIRS) * LEVELS, blocks // across, BLK * BLK, LANES)
    total = None
    for by in range(blocks // across):
        block = by * across + lax.broadcasted_iota(jnp.int32, (blocks, LANES), 1) // BLK
        mine = jnp.sum(jnp.where(index == block, named, 0), axis=0, keepdims=True)
        earlier = jnp.where((index < block) & (named == mine), 1, 0)
        slot = mine * cap + jnp.sum(earlier, axis=0, keepdims=True)
        chosen = jnp.where(slot_row == slot, 1.0, 0.0)
        payload = stresses[:, by].reshape(-1, LANES)
        part = lax.dot_general(
            chosen, payload, (((1,), (1,)), ((), ())), precision=HIGHEST, preferred_element_type=jnp.float32
        )
        total = part if total is None else total + part
    for d in range(outgoing.shape[0]):
        outgoing[d] = total[d * cap : (d + 1) * cap]


def call(kernel, out_shape, *args, scratch=(), hbm=0):
    whole = pl.BlockSpec(memory_space=pltpu.VMEM)
    return pl.pallas_call(
        kernel,
        out_shape=out_shape,
        in_specs=[pl.BlockSpec(memory_space=pl.ANY)] * hbm + [whole] * (len(args) - hbm),
        out_specs=jax.tree.map(lambda _: whole, out_shape),
        scratch_shapes=list(scratch),
        compiler_params=pltpu.CompilerParams(vmem_limit_bytes=VMEM_BYTES),
    )(*args)


def f32(*shape):
    return jax.ShapeDtypeStruct(shape, jnp.float32)


def per_device(fields, owner):
    _, _, height, width = fields.shape
    tiles = width // LANES
    places = TERMS * LEVELS
    rows = places * ROWS
    flat = fields.reshape(COMPONENTS * LEVELS, height, width)
    weights = jnp.asarray(east_weights(width))
    edge_at = jnp.asarray(edge_places())

    def tile_buffers(count):
        return [
            pltpu.VMEM((count, COMPONENTS * LEVELS, height, LANES), jnp.float32),
            pltpu.SemaphoreType.DMA((count,)),
        ]

    side_inner, side_edge, messages = call(
        side_kernel,
        (f32(2, rows, LANES), f32(2, 2 * places, LANES), f32(2, 8, rows + 2 * places)),
        flat,
        jnp.asarray(beyond_weights()),
        scratch=tile_buffers(2),
        hbm=1,
    )
    nx, ny = lax.axis_size("gx"), lax.axis_size("gy")
    up_x = [(i, (i + 1) % nx) for i in range(nx)]
    down_x = [(j, i) for i, j in up_x]
    up_y = [(i, (i + 1) % ny) for i in range(ny)]
    down_y = [(j, i) for i, j in up_y]
    from_east = lax.ppermute(messages[0], "gx", down_x)
    from_west = lax.ppermute(messages[1], "gx", up_x)
    inner, edge = call(
        inner_kernel,
        (f32(tiles - 2, rows, LANES), f32(tiles - 2, 2 * places, LANES)),
        flat,
        scratch=tile_buffers(tiles - 2),
        hbm=1,
    )
    before, after = call(
        edge_kernel, (f32(places, LANES), f32(places, LANES)), side_edge, edge, weights, edge_at, from_east, from_west
    )
    from_north = lax.ppermute(before, "gy", down_y)
    from_south = lax.ppermute(after, "gy", up_y)
    coarse = call(coarse_kernel, f32(rows, LANES), side_inner, inner, weights, edge_at, from_east, from_west)
    devices = nx * ny
    blocks = owner.shape[0]
    cap = max(2, 2 * blocks // devices)
    pay = len(PRODUCT_PAIRS) * LEVELS * BLK * BLK
    outgoing = call(
        functools.partial(send_kernel, cap),
        f32(devices, cap, pay),
        coarse,
        from_north,
        from_south,
        owner,
        scratch=[pltpu.VMEM((rows, LANES), jnp.float32), pltpu.VMEM((pay * blocks * BLK // LANES, LANES), jnp.float32)],
    )
    arrived = lax.all_to_all(outgoing, ("gx", "gy"), split_axis=0, concat_axis=0, tiled=True)
    return arrived.reshape(devices * cap, pay)


def solution(mesh):
    placed = (P(None, None, "gy", "gx"), P(("gx", "gy"), None))
    return jax.shard_map(
        per_device, mesh=mesh, in_specs=placed, out_specs=P(("gx", "gy"), None), check_vma=False
    )
```

```python
import functools

import jax
import jax.numpy as jnp
import numpy as np
from jax import lax
from jax.experimental import pallas as pl
from jax.experimental.pallas import tpu as pltpu
from jax.sharding import PartitionSpec as P

BLK = 4
RATIO = 10
LANES = 128
HIGHEST = lax.Precision.HIGHEST
SIGMA_CELLS = 2.8867513
PRODUCT_PAIRS = ((0, 0), (0, 1), (0, 2), (0, 3), (1, 1), (1, 2), (1, 3), (2, 2), (2, 3), (3, 3))
COMPONENTS = 4
TERMS = COMPONENTS + len(PRODUCT_PAIRS)
LEVELS = 4
ROWS = 8
EARLY = 4
VMEM_BYTES = 24 * 1024 * 1024


def gauss_taps():
    spread = np.arange(21, dtype=np.float64) - 10.0
    values = np.exp(-spread * spread / (2.0 * SIGMA_CELLS * SIGMA_CELLS))
    return (values / values.sum()).astype(np.float32)


TAPS = gauss_taps()
G = [float(v) for v in TAPS]


def east_weights(columns):
    fine = np.arange(columns)[:, None]
    coarse = np.arange(columns // RATIO)[None, :]
    tap = fine - RATIO * coarse + 5
    inside = (tap >= 0) & (tap <= 20)
    return np.where(inside, TAPS[np.clip(tap, 0, 20)], np.float32(0))


def beyond_weights(side):
    row = lax.broadcasted_iota(jnp.int32, (8, LANES), 0)
    lane = lax.broadcasted_iota(jnp.int32, (8, LANES), 1)
    weights = jnp.zeros((8, LANES), jnp.float32)
    for at, tap in enumerate(G[15:21]) if side == 0 else enumerate(G[0:5], LANES - 5):
        weights = jnp.where((row == 0) & (lane == at), tap, weights)
    return weights


def edge_places():
    places = np.zeros((16, LANES), np.float32)
    places[0, LANES - 1] = 1.0
    places[8, 0] = 1.0
    return places


def north_tile(field, level, store):
    def loads(p):
        return [field[c * LEVELS + level, pl.ds(p, ROWS, stride=RATIO), :] for c in range(COMPONENTS)]

    def weighed(values, weight, sums):
        scaled = [v * weight for v in values]
        terms = scaled + [scaled[a] * values[b] for a, b in PRODUCT_PAIRS]
        return terms if sums is None else [s + t for s, t in zip(sums, terms)]

    own = below = above = None
    for p in range(RATIO):
        values = loads(p)
        own = weighed(values, G[p + 5], own)
        if p <= 5:
            below = weighed(values, G[p + 15], below)
        if p >= 5:
            above = weighed(values, G[p - 5], above)
    row = lax.broadcasted_iota(jnp.int32, (ROWS, LANES), 0)
    for q in range(TERMS):
        from_next = jnp.where(row < ROWS - 1, pltpu.roll(below[q], ROWS - 1, 0), 0.0)
        from_last = jnp.where(row > 0, pltpu.roll(above[q], 1, 0), 0.0)
        store(q * LEVELS + level, own[q] + from_next + from_last, below[q][0:1, :], above[q][ROWS - 1 : ROWS, :])


def store_in(inner, edge, lead):
    def store(place, inside, before, after):
        inner[lead, pl.ds(place * ROWS, ROWS), :] = inside
        edge[lead, pl.ds(place, 1), :] = before
        edge[lead, pl.ds(TERMS * LEVELS + place, 1), :] = after

    return store


def tile_copies(fields, places, sems):
    return [
        pltpu.make_async_copy(fields.at[:, :, pl.ds(t * LANES, LANES)], place, sems.at[t]) for t, place in places
    ]


def early_kernel(order, fields, inner, edge, message, later, tile, sems):
    places = [(t, tile.at[i] if i < EARLY else later.at[i - EARLY]) for i, t in enumerate(order)]
    copies = tile_copies(fields, places, sems)
    for copy in copies:
        copy.start()
    for i in range(EARLY):
        copies[i].wait()
        for level in range(LEVELS):
            north_tile(tile.at[i], level, store_in(inner, edge, i))
        if i < 2:
            sums = jnp.concatenate([inner[i], edge[i]], axis=0)
            message[i] = lax.dot_general(
                beyond_weights(i), sums, (((1,), (1,)), ((), ())), precision=HIGHEST, preferred_element_type=jnp.float32
            )
    for copy in copies[EARLY:]:
        copy.wait()


def later_kernel(tile, inner, edge):
    def step(t, carry):
        for level in range(LEVELS):
            north_tile(tile.at[t], level, store_in(inner, edge, t))
        return carry

    lax.fori_loop(0, tile.shape[0], step, 0)


def east_sums(order, early, later, weights):
    tiles = [early[t] for t in range(EARLY)] + [later[t] for t in range(len(order) - EARLY)]
    total = None
    for i in range(0, len(order), 2):
        pair = jnp.concatenate(tiles[i : i + 2], axis=1)
        rows = jnp.concatenate([weights[t * LANES : (t + 1) * LANES, :] for t in order[i : i + 2]], axis=0)
        part = jnp.dot(pair, rows, precision=HIGHEST, preferred_element_type=jnp.float32)
        total = part if total is None else total + part
    return total


def from_sides(east, west, places):
    both = jnp.concatenate([east, west], axis=0)
    return lax.dot_general(
        both, places[...], (((0,), (0,)), ((), ())), precision=HIGHEST, preferred_element_type=jnp.float32
    )


def edge_kernel(order, early, later, weights, places, west, east, before, after):
    start = TERMS * LEVELS * ROWS
    total = east_sums(order, early, later, weights) + from_sides(east[:, start:], west[:, start:], places)
    half = TERMS * LEVELS
    before[...] = total[:half]
    after[...] = total[half:]


def coarse_kernel(order, early, later, weights, places, west, east, coarse):
    stop = TERMS * LEVELS * ROWS
    coarse[...] = east_sums(order, early, later, weights) + from_sides(east[:, :stop], west[:, :stop], places)


def send_kernel(cap, coarse, south, north, owner, outgoing, filtered, spread):
    filtered[...] = coarse[...]
    half = TERMS * LEVELS
    filtered[pl.ds(0, half, stride=ROWS), :] += south[...]
    filtered[pl.ds(ROWS - 1, half, stride=ROWS), :] += north[...]
    slab = LEVELS * ROWS
    means = [filtered[c * slab : (c + 1) * slab, :] for c in range(COMPONENTS)]
    lane = lax.broadcasted_iota(jnp.int32, (slab, LANES), 1) % BLK
    for k, (a, b) in enumerate(PRODUCT_PAIRS):
        q = COMPONENTS + k
        stress = filtered[q * slab : (q + 1) * slab, :] - means[a] * means[b]
        for c in range(BLK):
            spread[pl.ds(k * slab * BLK + c, slab, stride=BLK), :] = jnp.where(lane == c, stress, 0.0)
    slots = outgoing.shape[0] * outgoing.shape[1]
    blocks = owner.shape[0]
    across = LANES // BLK
    index = lax.broadcasted_iota(jnp.int32, (blocks, LANES), 0)
    named = jnp.broadcast_to(owner[...], (blocks, LANES))
    slot_row = lax.broadcasted_iota(jnp.int32, (slots, LANES), 0)
    stresses = spread[...].reshape(len(PRODUCT_PAIRS) * LEVELS, blocks // across, BLK * BLK, LANES)
    total = None
    for by in range(blocks // across):
        block = by * across + lax.broadcasted_iota(jnp.int32, (blocks, LANES), 1) // BLK
        mine = jnp.sum(jnp.where(index == block, named, 0), axis=0, keepdims=True)
        earlier = jnp.where((index < block) & (named == mine), 1, 0)
        slot = mine * cap + jnp.sum(earlier, axis=0, keepdims=True)
        chosen = jnp.where(slot_row == slot, 1.0, 0.0)
        payload = stresses[:, by].reshape(-1, LANES)
        part = lax.dot_general(
            chosen, payload, (((1,), (1,)), ((), ())), precision=HIGHEST, preferred_element_type=jnp.float32
        )
        total = part if total is None else total + part
    for d in range(outgoing.shape[0]):
        outgoing[d] = total[d * cap : (d + 1) * cap]


def call(kernel, out_shape, *args, scratch=(), hbm=0):
    whole = pl.BlockSpec(memory_space=pltpu.VMEM)
    return pl.pallas_call(
        kernel,
        out_shape=out_shape,
        in_specs=[pl.BlockSpec(memory_space=pltpu.HBM)] * hbm + [whole] * (len(args) - hbm),
        out_specs=jax.tree.map(lambda _: whole, out_shape),
        scratch_shapes=list(scratch),
        compiler_params=pltpu.CompilerParams(vmem_limit_bytes=VMEM_BYTES),
    )(*args)


def f32(*shape):
    return jax.ShapeDtypeStruct(shape, jnp.float32)


def per_device(fields, owner):
    _, _, height, width = fields.shape
    tiles = width // LANES
    places = TERMS * LEVELS
    rows = places * ROWS
    flat = fields.reshape(COMPONENTS * LEVELS, height, width)
    weights = jnp.asarray(east_weights(width))
    edge_at = jnp.asarray(edge_places())

    order = (0, tiles - 1) + tuple(range(1, tiles - 1))
    rest = tiles - EARLY
    early_inner, early_edge, messages, later = call(
        functools.partial(early_kernel, order),
        (
            f32(EARLY, rows, LANES),
            f32(EARLY, 2 * places, LANES),
            f32(2, 8, rows + 2 * places),
            f32(rest, COMPONENTS * LEVELS, height, LANES),
        ),
        pltpu.with_memory_space_constraint(flat, pltpu.HBM),
        scratch=[
            pltpu.VMEM((EARLY, COMPONENTS * LEVELS, height, LANES), jnp.float32),
            pltpu.SemaphoreType.DMA((tiles,)),
        ],
        hbm=1,
    )
    nx, ny = lax.axis_size("gx"), lax.axis_size("gy")
    up_x = [(i, (i + 1) % nx) for i in range(nx)]
    down_x = [(j, i) for i, j in up_x]
    up_y = [(i, (i + 1) % ny) for i in range(ny)]
    down_y = [(j, i) for i, j in up_y]
    from_west = lax.ppermute(messages[1], "gx", up_x)
    from_east = lax.ppermute(messages[0], "gx", down_x)
    later_inner, later_edge = call(later_kernel, (f32(rest, rows, LANES), f32(rest, 2 * places, LANES)), later)
    before, after = call(
        functools.partial(edge_kernel, order),
        (f32(places, LANES), f32(places, LANES)),
        early_edge,
        later_edge,
        weights,
        edge_at,
        from_west,
        from_east,
    )
    from_south = lax.ppermute(after, "gy", up_y)
    from_north = lax.ppermute(before, "gy", down_y)
    coarse = call(
        functools.partial(coarse_kernel, order),
        f32(rows, LANES),
        early_inner,
        later_inner,
        weights,
        edge_at,
        from_west,
        from_east,
    )
    devices = nx * ny
    blocks = owner.shape[0]
    cap = max(2, 2 * blocks // devices)
    pay = len(PRODUCT_PAIRS) * LEVELS * BLK * BLK
    outgoing = call(
        functools.partial(send_kernel, cap),
        f32(devices, cap, pay),
        coarse,
        from_south,
        from_north,
        owner,
        scratch=[pltpu.VMEM((rows, LANES), jnp.float32), pltpu.VMEM((pay * blocks * BLK // LANES, LANES), jnp.float32)],
    )
    arrived = lax.all_to_all(outgoing, ("gx", "gy"), split_axis=0, concat_axis=0, tiled=True)
    return arrived.reshape(devices * cap, pay)


def solution(mesh):
    placed = (P(None, None, "gy", "gx"), P(("gx", "gy"), None))
    return jax.shard_map(
        per_device, mesh=mesh, in_specs=placed, out_specs=P(("gx", "gy"), None), check_vma=False
    )
```

```python
import functools

import jax
import jax.numpy as jnp
import numpy as np
from jax import lax
from jax.experimental import pallas as pl
from jax.experimental.pallas import tpu as pltpu
from jax.sharding import PartitionSpec as P

BLK = 4
RATIO = 10
LANES = 128
HIGHEST = lax.Precision.HIGHEST
SIGMA_CELLS = 2.8867513
PRODUCT_PAIRS = ((0, 0), (0, 1), (0, 2), (0, 3), (1, 1), (1, 2), (1, 3), (2, 2), (2, 3), (3, 3))
COMPONENTS = 4
TERMS = COMPONENTS + len(PRODUCT_PAIRS)
LEVELS = 4
ROWS = 8
OUTER = 2
READY = 3
PADDED = 16
EDGE = LEVELS * PADDED
VMEM_BYTES = 16 * 1024 * 1024


def gauss_taps():
    spread = np.arange(21, dtype=np.float64) - 10.0
    values = np.exp(-spread * spread / (2.0 * SIGMA_CELLS * SIGMA_CELLS))
    return (values / values.sum()).astype(np.float32)


TAPS = gauss_taps()
G = [float(v) for v in TAPS]


def east_weights(columns):
    fine = np.arange(columns)[:, None]
    coarse = np.arange(columns // RATIO)[None, :]
    tap = fine - RATIO * coarse + 5
    inside = (tap >= 0) & (tap <= 20)
    return np.where(inside, TAPS[np.clip(tap, 0, 20)], np.float32(0))


def beyond_weights(side):
    row = lax.broadcasted_iota(jnp.int32, (8, LANES), 0)
    lane = lax.broadcasted_iota(jnp.int32, (8, LANES), 1)
    weights = jnp.zeros((8, LANES), jnp.float32)
    for at, tap in enumerate(G[15:21]) if side == 0 else enumerate(G[0:5], LANES - 5):
        weights = jnp.where((row == 0) & (lane == at), tap, weights)
    return weights


def edge_places():
    odd = lax.axis_index("gx") % 2
    row = lax.broadcasted_iota(jnp.int32, (16, LANES), 0)
    lane = lax.broadcasted_iota(jnp.int32, (16, LANES), 1)
    across = odd * (LANES - 1)
    return jnp.where((row == 0) & (lane == across) | (row == 8) & (lane == LANES - 1 - across), 1.0, 0.0)


def weighed(values, weight, sums):
    scaled = [v * weight for v in values]
    terms = scaled + [scaled[a] * values[b] for a, b in PRODUCT_PAIRS]
    return terms if sums is None else [s + t for s, t in zip(sums, terms)]


def north_sums(load):
    own = below = above = None
    for p in range(RATIO):
        values = load(p)
        own = weighed(values, G[p + 5], own)
        if p <= 5:
            below = weighed(values, G[p + 15], below)
        if p >= 5:
            above = weighed(values, G[p - 5], above)
    row = lax.broadcasted_iota(jnp.int32, (ROWS, LANES), 0)
    inside = []
    for q in range(TERMS):
        from_next = jnp.where(row < ROWS - 1, pltpu.roll(below[q], ROWS - 1, 0), 0.0)
        from_last = jnp.where(row > 0, pltpu.roll(above[q], 1, 0), 0.0)
        inside.append(own[q] + from_next + from_last)
    return inside, below, above


def strided(tile, level, p):
    return [tile[c * LEVELS + level, pl.ds(p, ROWS, stride=RATIO), :] for c in range(COMPONENTS)]


def sublane_sums(values):
    row = lax.broadcasted_iota(jnp.int32, (ROWS, LANES), 0)

    def fours(a, b):
        return jnp.where(row < 4, a, b) + pltpu.roll(jnp.where(row < 4, b, a), 4, 0)

    def fewer(a, b, step):
        return jnp.where(row & step == 0, a + pltpu.roll(a, ROWS - step, 0), b + pltpu.roll(b, step, 0))

    u = [fours(values[i], values[i + 4]) for i in range(4)]
    return fewer(fewer(u[0], u[2], 2), fewer(u[1], u[3], 2), 1)


def end_taps(side):
    row = lax.broadcasted_iota(jnp.int32, (ROWS, LANES), 0)
    column = jnp.zeros((ROWS, LANES), jnp.float32)
    for r, tap in enumerate(G[15:21]) if side == 0 else enumerate(G[0:5], ROWS - 5):
        column = jnp.where(row == r, tap, column)
    return column


def end_sums(tile, edge):
    last = tile.shape[1] - ROWS
    for side, start in enumerate((0, last)):
        taps = end_taps(side)
        for level in range(LEVELS):
            values = [tile[c * LEVELS + level, pl.ds(start, ROWS), :] for c in range(COMPONENTS)]
            terms = weighed(values, taps, None)
            place = side * EDGE + level * PADDED
            edge[pl.ds(place, ROWS), :] = sublane_sums(terms[:ROWS])
            edge[pl.ds(place + ROWS, ROWS), :] = sublane_sums(terms[ROWS:] + terms[: 2 * ROWS - TERMS])


def filter_tile(tile, inner, edge=None):
    for level in range(LEVELS):
        inside, below, above = north_sums(functools.partial(strided, tile, level))
        for q in range(TERMS):
            inner[pl.ds((q * LEVELS + level) * ROWS, ROWS), :] = inside[q]
            if edge is not None:
                edge[pl.ds(level * PADDED + q, 1), :] = below[q][0:1]
                edge[pl.ds(EDGE + level * PADDED + q, 1), :] = above[q][ROWS - 1 : ROWS]


def clear_padding(edge):
    for level in range(2 * LEVELS):
        edge[pl.ds(level * PADDED + ROWS, ROWS), :] = jnp.zeros((ROWS, LANES), jnp.float32)


def tile_copies(fields, places, sems):
    return [
        pltpu.make_async_copy(fields.at[:, :, pl.ds(t * LANES, LANES)], place, sems.at[i])
        for i, (t, place) in enumerate(places)
    ]


def outer_kernel(order, fields, inner, edge, across, beside, ready, tile, sems):
    places = [(t, tile.at[i] if i < OUTER else ready.at[i - OUTER]) for i, t in enumerate(order[: OUTER + READY])]
    copies = tile_copies(fields, places, sems)
    for copy in copies:
        copy.start()
    messages = []
    for i in range(OUTER):
        clear_padding(edge.at[i])
        copies[i].wait()
        filter_tile(tile.at[i], inner.at[i], edge.at[i])
        sums = jnp.concatenate([inner[i], edge[i]], axis=0)
        messages.append(
            lax.dot_general(
                beyond_weights(i), sums, (((1,), (1,)), ((), ())), precision=HIGHEST, preferred_element_type=jnp.float32
            )
        )
    odd = lax.axis_index("gx") % 2 == 1
    across[...] = jnp.where(odd, messages[1], messages[0])
    beside[...] = jnp.where(odd, messages[0], messages[1])
    for copy in copies[OUTER:]:
        copy.wait()


def middle_kernel(order, fields, outer_edge, ready, weights, inner, partial, later, edge, sems):
    count = len(order) - OUTER - READY
    copies = tile_copies(fields, [(t, later.at[i]) for i, t in enumerate(order[OUTER + READY :])], sems)
    for copy in copies:
        copy.start()
    for i in range(READY):
        clear_padding(edge.at[i])
        filter_tile(ready.at[i], inner.at[i], edge.at[i])
    for i in range(count):
        copies[i].wait()
        end_sums(later.at[i], edge.at[READY + i])
    tiles = [outer_edge[i] for i in range(OUTER)] + [edge[i] for i in range(READY + count)]
    partial[...] = east_sums(order, tiles, weights)


def east_sums(order, tiles, weights):
    total = None
    for i in range(0, len(order), 2):
        pair = jnp.concatenate(tiles[i : i + 2], axis=1)
        rows = jnp.concatenate([weights[t * LANES : (t + 1) * LANES, :] for t in order[i : i + 2]], axis=0)
        part = jnp.dot(pair, rows, precision=HIGHEST, preferred_element_type=jnp.float32)
        total = part if total is None else total + part
    return total


def from_sides(across, beside):
    both = jnp.concatenate([across, beside], axis=0)
    return lax.dot_general(
        both, edge_places(), (((0,), (0,)), ((), ())), precision=HIGHEST, preferred_element_type=jnp.float32
    )


def corner_kernel(partial, across, beside, before, after):
    start = TERMS * LEVELS * ROWS
    total = partial[...] + from_sides(across[:, start:], beside[:, start:])
    before[...] = total[:EDGE]
    after[...] = total[EDGE:]


def coarse_kernel(order, outer_inner, ready_inner, later, weights, across, beside, coarse, inner):
    count = later.shape[0]
    for i in range(count):
        filter_tile(later.at[i], inner.at[i])
    tiles = [outer_inner[i] for i in range(OUTER)] + [ready_inner[i] for i in range(READY)]
    tiles += [inner[i] for i in range(count)]
    stop = TERMS * LEVELS * ROWS
    coarse[...] = east_sums(order, tiles, weights) + from_sides(across[:, :stop], beside[:, :stop])


def send_kernel(cap, coarse, south, north, owner, outgoing, filtered, spread):
    filtered[...] = coarse[...]
    slab = LEVELS * ROWS
    for level in range(LEVELS):
        filtered[pl.ds(level * ROWS, TERMS, stride=slab), :] += south[pl.ds(level * PADDED, TERMS), :]
        filtered[pl.ds(level * ROWS + ROWS - 1, TERMS, stride=slab), :] += north[pl.ds(level * PADDED, TERMS), :]
    means = [filtered[c * slab : (c + 1) * slab, :] for c in range(COMPONENTS)]
    lane = lax.broadcasted_iota(jnp.int32, (slab, LANES), 1) % BLK
    for k, (a, b) in enumerate(PRODUCT_PAIRS):
        q = COMPONENTS + k
        stress = filtered[q * slab : (q + 1) * slab, :] - means[a] * means[b]
        for c in range(BLK):
            spread[pl.ds(k * slab * BLK + c, slab, stride=BLK), :] = jnp.where(lane == c, stress, 0.0)
    slots = outgoing.shape[0] * outgoing.shape[1]
    blocks = owner.shape[1]
    across = LANES // BLK
    own = lax.broadcasted_iota(jnp.int32, (blocks, blocks), 0) == lax.broadcasted_iota(jnp.int32, (blocks, blocks), 1)
    column = jnp.sum(jnp.where(own, jnp.broadcast_to(owner[...], (blocks, blocks)), 0), axis=1, keepdims=True)
    index = lax.broadcasted_iota(jnp.int32, (blocks, LANES), 0)
    named = jnp.broadcast_to(column, (blocks, LANES))
    slot_row = lax.broadcasted_iota(jnp.int32, (slots, LANES), 0)
    stresses = spread[...].reshape(len(PRODUCT_PAIRS) * LEVELS, blocks // across, BLK * BLK, LANES)
    total = None
    for by in range(blocks // across):
        block = by * across + lax.broadcasted_iota(jnp.int32, (blocks, LANES), 1) // BLK
        mine = jnp.sum(jnp.where(index == block, named, 0), axis=0, keepdims=True)
        earlier = jnp.where((index < block) & (named == mine), 1, 0)
        slot = mine * cap + jnp.sum(earlier, axis=0, keepdims=True)
        chosen = jnp.where(slot_row == slot, 1.0, 0.0)
        payload = stresses[:, by].reshape(-1, LANES)
        part = lax.dot_general(
            chosen, payload, (((1,), (1,)), ((), ())), precision=HIGHEST, preferred_element_type=jnp.float32
        )
        total = part if total is None else total + part
    for d in range(outgoing.shape[0]):
        outgoing[d] = total[d * cap : (d + 1) * cap]


def call(kernel, out_shape, *args, scratch=(), hbm=0):
    whole = pl.BlockSpec(memory_space=pltpu.VMEM)
    held = [pltpu.with_memory_space_constraint(a, pltpu.VMEM if i >= hbm else pltpu.HBM) for i, a in enumerate(args)]
    return pl.pallas_call(
        kernel,
        out_shape=out_shape,
        in_specs=[pl.BlockSpec(memory_space=pltpu.HBM)] * hbm + [whole] * (len(args) - hbm),
        out_specs=jax.tree.map(lambda _: whole, out_shape),
        scratch_shapes=list(scratch),
        compiler_params=pltpu.CompilerParams(vmem_limit_bytes=VMEM_BYTES),
    )(*held)


def f32(*shape):
    return jax.ShapeDtypeStruct(shape, jnp.float32)


def per_device(fields, owner):
    _, _, height, width = fields.shape
    tiles = width // LANES
    rows = TERMS * LEVELS * ROWS
    fine = COMPONENTS * LEVELS
    flat = fields.reshape(fine, height, width)
    weights = jnp.asarray(east_weights(width))
    order = (0, tiles - 1) + tuple(range(1, tiles - 1))
    rest = tiles - OUTER - READY
    message = f32(8, rows + 2 * EDGE)
    outer_inner, outer_edge, to_across, to_beside, ready = call(
        functools.partial(outer_kernel, order),
        (
            f32(OUTER, rows, LANES),
            f32(OUTER, 2 * EDGE, LANES),
            message,
            message,
            f32(READY, fine, height, LANES),
        ),
        flat,
        scratch=[pltpu.VMEM((OUTER, fine, height, LANES), jnp.float32), pltpu.SemaphoreType.DMA((OUTER + READY,))],
        hbm=1,
    )
    nx, ny = lax.axis_size("gx"), lax.axis_size("gy")
    beside_x = [(i, i ^ 1) for i in range(nx)]
    across_x = [(i, (i + 1) % nx if i % 2 else (i - 1) % nx) for i in range(nx)]
    up_y = [(i, (i + 1) % ny) for i in range(ny)]
    down_y = [(j, i) for i, j in up_y]
    across = lax.ppermute(to_across, "gx", across_x)
    beside = lax.ppermute(to_beside, "gx", beside_x)
    ready_inner, partial, later = call(
        functools.partial(middle_kernel, order),
        (f32(READY, rows, LANES), f32(2 * EDGE, LANES), f32(rest, fine, height, LANES)),
        flat,
        outer_edge,
        ready,
        weights,
        scratch=[pltpu.VMEM((READY + rest, 2 * EDGE, LANES), jnp.float32), pltpu.SemaphoreType.DMA((rest,))],
        hbm=1,
    )
    before, after = call(corner_kernel, (f32(EDGE, LANES), f32(EDGE, LANES)), partial, across, beside)
    from_south = lax.ppermute(after, "gy", up_y)
    from_north = lax.ppermute(before, "gy", down_y)
    coarse = call(
        functools.partial(coarse_kernel, order),
        f32(rows, LANES),
        outer_inner,
        ready_inner,
        later,
        weights,
        across,
        beside,
        scratch=[pltpu.VMEM((rest, rows, LANES), jnp.float32)],
    )
    devices = nx * ny
    blocks = owner.shape[0]
    cap = max(2, 2 * blocks // devices)
    pay = len(PRODUCT_PAIRS) * LEVELS * BLK * BLK
    outgoing = call(
        functools.partial(send_kernel, cap),
        f32(devices, cap, pay),
        coarse,
        from_south,
        from_north,
        owner.reshape(1, blocks),
        scratch=[pltpu.VMEM((rows, LANES), jnp.float32), pltpu.VMEM((pay * blocks * BLK // LANES, LANES), jnp.float32)],
    )
    arrived = lax.all_to_all(outgoing, ("gx", "gy"), split_axis=0, concat_axis=0, tiled=True)
    return arrived.reshape(devices * cap, pay)


def solution(mesh):
    placed = (P(None, None, "gy", "gx"), P(("gx", "gy"), None))
    return jax.shard_map(
        per_device, mesh=mesh, in_specs=placed, out_specs=P(("gx", "gy"), None), check_vma=False
    )
```

```python
import functools

import jax
import jax.numpy as jnp
import ml_dtypes
import numpy as np
from jax import lax
from jax.experimental import pallas as pl
from jax.experimental.pallas import tpu as pltpu
from jax.sharding import PartitionSpec as P

BLK = 4
RATIO = 10
LANES = 128
HIGHEST = lax.Precision.HIGHEST
SIGMA_CELLS = 2.8867513
PRODUCT_PAIRS = ((0, 0), (0, 1), (0, 2), (0, 3), (1, 1), (1, 2), (1, 3), (2, 2), (2, 3), (3, 3))
COMPONENTS = 4
TERMS = COMPONENTS + len(PRODUCT_PAIRS)
LEVELS = 4
ROWS = 8
OUTER = 2
READY = 3
PADDED = 16
EDGE = LEVELS * PADDED
VMEM_BYTES = 16 * 1024 * 1024


def gauss_taps():
    spread = np.arange(21, dtype=np.float64) - 10.0
    values = np.exp(-spread * spread / (2.0 * SIGMA_CELLS * SIGMA_CELLS))
    return (values / values.sum()).astype(np.float32)


TAPS = gauss_taps()
G = [float(v) for v in TAPS]


def east_weights(columns):
    fine = np.arange(columns)[:, None]
    coarse = np.arange(columns // RATIO)[None, :]
    tap = fine - RATIO * coarse + 5
    inside = (tap >= 0) & (tap <= 20)
    return np.where(inside, TAPS[np.clip(tap, 0, 20)], np.float32(0))


def split(values):
    parts = []
    for _ in range(3):
        part = values.astype(ml_dtypes.bfloat16)
        parts.append(part)
        values = values - part.astype(np.float32)
    return parts


def split_weights(columns, order):
    tiles = east_weights(columns).reshape(-1, LANES, columns // RATIO)
    first, second, third = split(tiles[list(order)].reshape(columns, -1))
    return np.concatenate([first, second], axis=1), third


def beyond_weights():
    row = lax.broadcasted_iota(jnp.int32, (16, LANES), 0)
    lane = lax.broadcasted_iota(jnp.int32, (16, LANES), 1)
    weights = jnp.zeros((16, LANES), jnp.float32)
    for side, taps in ((0, enumerate(G[15:21])), (8, enumerate(G[0:5], LANES - 5))):
        for at, tap in taps:
            weights = jnp.where((row == side) & (lane == at), tap, weights)
    return weights


def edge_places():
    odd = lax.axis_index("gx") % 2
    row = lax.broadcasted_iota(jnp.int32, (16, LANES), 0)
    lane = lax.broadcasted_iota(jnp.int32, (16, LANES), 1)
    across = odd * (LANES - 1)
    return jnp.where((row == 0) & (lane == across) | (row == 8) & (lane == LANES - 1 - across), 1.0, 0.0)


def weighed(values, weight, sums):
    scaled = [v * weight for v in values]
    terms = scaled + [scaled[a] * values[b] for a, b in PRODUCT_PAIRS]
    return terms if sums is None else [s + t for s, t in zip(sums, terms)]


def north_sums(load):
    own = below = above = None
    for p in range(RATIO):
        values = load(p)
        own = weighed(values, G[p + 5], own)
        if p <= 5:
            below = weighed(values, G[p + 15], below)
        if p >= 5:
            above = weighed(values, G[p - 5], above)
    row = lax.broadcasted_iota(jnp.int32, (ROWS, LANES), 0)
    inside = []
    for q in range(TERMS):
        from_next = jnp.where(row < ROWS - 1, pltpu.roll(below[q], ROWS - 1, 0), 0.0)
        from_last = jnp.where(row > 0, pltpu.roll(above[q], 1, 0), 0.0)
        inside.append(own[q] + from_next + from_last)
    return inside, below, above


def strided(tile, level, p):
    return [tile[c, level, pl.ds(p, ROWS, stride=RATIO), :] for c in range(COMPONENTS)]


def sublane_sums(values):
    row = lax.broadcasted_iota(jnp.int32, (ROWS, LANES), 0)

    def fours(a, b):
        return jnp.where(row < 4, a, b) + pltpu.roll(jnp.where(row < 4, b, a), 4, 0)

    def fewer(a, b, step):
        return jnp.where(row & step == 0, a + pltpu.roll(a, ROWS - step, 0), b + pltpu.roll(b, step, 0))

    u = [fours(values[i], values[i + 4]) for i in range(4)]
    return fewer(fewer(u[0], u[2], 2), fewer(u[1], u[3], 2), 1)


def end_taps(side):
    row = lax.broadcasted_iota(jnp.int32, (ROWS, LANES), 0)
    column = jnp.zeros((ROWS, LANES), jnp.float32)
    for r, tap in enumerate(G[15:21]) if side == 0 else enumerate(G[0:5], ROWS - 5):
        column = jnp.where(row == r, tap, column)
    return column


def end_sums(tile, edge):
    last = tile.shape[2] - ROWS
    for side, start in enumerate((0, last)):
        taps = end_taps(side)
        for level in range(LEVELS):
            values = [tile[c, level, pl.ds(start, ROWS), :] for c in range(COMPONENTS)]
            terms = weighed(values, taps, None)
            place = side * EDGE + level * PADDED
            edge[pl.ds(place, ROWS), :] = sublane_sums(terms[:ROWS])
            edge[pl.ds(place + ROWS, ROWS), :] = sublane_sums(terms[ROWS:] + terms[: 2 * ROWS - TERMS])


def filter_level(tile, level, inner, edge=None):
    inside, below, above = north_sums(functools.partial(strided, tile, level))
    for q in range(TERMS):
        inner[pl.ds((q * LEVELS + level) * ROWS, ROWS), :] = inside[q]
        if edge is not None:
            edge[pl.ds(level * PADDED + q, 1), :] = below[q][0:1]
            edge[pl.ds(EDGE + level * PADDED + q, 1), :] = above[q][ROWS - 1 : ROWS]


def clear_padding(edge):
    for level in range(2 * LEVELS):
        edge[pl.ds(level * PADDED + ROWS, ROWS), :] = jnp.zeros((ROWS, LANES), jnp.float32)


def tile_copies(fields, places, sems):
    return [
        pltpu.make_async_copy(fields.at[:, :, :, pl.ds(t * LANES, LANES)], place, sems.at[i])
        for i, (t, place) in enumerate(places)
    ]


def outer_kernel(order, fields, inner, edge, across, beside, ready, tile, level_sems, sems):
    arriving = [
        [
            pltpu.make_async_copy(
                fields.at[:, level, :, pl.ds(order[i] * LANES, LANES)], tile.at[i, :, level], level_sems.at[i, level]
            )
            for level in range(LEVELS)
        ]
        for i in range(OUTER)
    ]
    copies = tile_copies(fields, [(t, ready.at[i]) for i, t in enumerate(order[OUTER : OUTER + READY])], sems)
    for copy in arriving[0] + arriving[1] + copies:
        copy.start()
    for i in range(OUTER):
        clear_padding(edge.at[i])
        for level in range(LEVELS):
            arriving[i][level].wait()
            filter_level(tile.at[i], level, inner.at[i], edge.at[i])
    lane = lax.broadcasted_iota(jnp.int32, (1, LANES), 1)
    first, last = (jnp.concatenate([inner[i], edge[i]], axis=0) for i in range(OUTER))
    beyond = jnp.concatenate(split_here(beyond_weights()), axis=0)
    total = None
    for part in split_here(jnp.where(lane < LANES // 2, first, last)):
        sums = lax.dot_general(beyond, part, (((1,), (1,)), ((), ())), preferred_element_type=jnp.float32)
        total = sums if total is None else total + sums
    messages = total[:16] + (total[16:32] + total[32:])
    odd = lax.axis_index("gx") % 2 == 1
    across[...] = jnp.where(odd, messages[8:], messages[:8])
    beside[...] = jnp.where(odd, messages[:8], messages[8:])
    for copy in copies:
        copy.wait()


def split_here(values):
    first = values.astype(jnp.bfloat16)
    left = values - first.astype(jnp.float32)
    second = left.astype(jnp.bfloat16)
    return first, second, (left - second.astype(jnp.float32)).astype(jnp.bfloat16)


def dot(a, b):
    return jnp.dot(a, b, preferred_element_type=jnp.float32)


def east_sums(values, pair, weights, third):
    rows = pl.ds(pair * 2 * LANES, 2 * LANES)
    a, b, c = split_here(values)
    both = dot(a, weights[rows, :]) + dot(b, weights[rows, :])
    small = dot(a, third[rows, :]) + dot(c, weights[rows, :LANES])
    return both[:, :LANES] + (both[:, LANES:] + small)


def middle_kernel(order, fields, outer_edge, ready, weights, third, inner, partial, later, edge, sems):
    count = len(order) - OUTER - READY
    copies = tile_copies(fields, [(t, later.at[i]) for i, t in enumerate(order[OUTER + READY :])], sems)
    for copy in copies:
        copy.start()
    tiles = [outer_edge.at[i] for i in range(OUTER)] + [edge.at[i] for i in range(READY + count)]

    def add(pair):
        both = jnp.concatenate([tiles[2 * pair][...], tiles[2 * pair + 1][...]], axis=1)
        part = east_sums(both, pair, weights, third)
        partial[...] = part if pair == 0 else partial[...] + part

    done = 0
    for i in range(READY + count):
        clear_padding(edge.at[i])
        if i < READY:
            for level in range(LEVELS):
                filter_level(ready.at[i], level, inner.at[i], edge.at[i])
        else:
            copies[i - READY].wait()
            end_sums(later.at[i - READY], edge.at[i])
        if 2 * done + 2 <= OUTER + i:
            add(done)
            done += 1
    for pair in range(done, len(order) // 2):
        add(pair)


def from_sides(across, beside):
    both = jnp.concatenate([across, beside], axis=0)
    return lax.dot_general(
        both, edge_places(), (((0,), (0,)), ((), ())), precision=HIGHEST, preferred_element_type=jnp.float32
    )


def corner_kernel(partial, across, beside, before, after):
    start = TERMS * LEVELS * ROWS
    total = partial[...] + from_sides(across[:, start:], beside[:, start:])
    before[...] = total[:EDGE]
    after[...] = total[EDGE:]


def coarse_kernel(outer_inner, ready_inner, later, weights, third, across, beside, coarse, inner):
    count = later.shape[0]
    tiles = [outer_inner.at[i] for i in range(OUTER)] + [ready_inner.at[i] for i in range(READY)]
    tiles += [inner.at[i] for i in range(count)]
    stop = TERMS * LEVELS * ROWS
    coarse[...] = from_sides(across[:, :stop], beside[:, :stop])

    def add(pair):
        both = jnp.concatenate([tiles[2 * pair][...], tiles[2 * pair + 1][...]], axis=1)
        coarse[...] += east_sums(both, pair, weights, third)

    done = 0
    for i in range(count):
        if 2 * done + 2 <= OUTER + READY + i:
            add(done)
            done += 1
        for level in range(LEVELS):
            filter_level(later.at[i], level, inner.at[i])
    for pair in range(done, len(tiles) // 2):
        add(pair)


def send_kernel(cap, coarse, south, north, owner, outgoing, filtered, spread):
    filtered[...] = coarse[...]
    slab = LEVELS * ROWS
    for level in range(LEVELS):
        filtered[pl.ds(level * ROWS, TERMS, stride=slab), :] += south[pl.ds(level * PADDED, TERMS), :]
        filtered[pl.ds(level * ROWS + ROWS - 1, TERMS, stride=slab), :] += north[pl.ds(level * PADDED, TERMS), :]
    means = [filtered[c * slab : (c + 1) * slab, :] for c in range(COMPONENTS)]
    lane = lax.broadcasted_iota(jnp.int32, (slab, LANES), 1) % BLK
    for k, (a, b) in enumerate(PRODUCT_PAIRS):
        q = COMPONENTS + k
        stress = filtered[q * slab : (q + 1) * slab, :] - means[a] * means[b]
        for c in range(BLK):
            spread[pl.ds(k * slab * BLK + c, slab, stride=BLK), :] = jnp.where(lane == c, stress, 0.0)
    slots = outgoing.shape[0] * outgoing.shape[1]
    blocks = owner.shape[1]
    across = LANES // BLK
    own = lax.broadcasted_iota(jnp.int32, (blocks, blocks), 0) == lax.broadcasted_iota(jnp.int32, (blocks, blocks), 1)
    column = jnp.sum(jnp.where(own, jnp.broadcast_to(owner[...], (blocks, blocks)), 0), axis=1, keepdims=True)
    index = lax.broadcasted_iota(jnp.int32, (blocks, LANES), 0)
    named = jnp.broadcast_to(column, (blocks, LANES))
    slot_row = lax.broadcasted_iota(jnp.int32, (slots, LANES), 0)
    stresses = spread[...].reshape(len(PRODUCT_PAIRS) * LEVELS, blocks // across, BLK * BLK, LANES)
    picks, payloads = [], []
    for by in range(blocks // across):
        block = by * across + lax.broadcasted_iota(jnp.int32, (blocks, LANES), 1) // BLK
        mine = jnp.sum(jnp.where(index == block, named, 0), axis=0, keepdims=True)
        earlier = jnp.where((index < block) & (named == mine), 1, 0)
        slot = mine * cap + jnp.sum(earlier, axis=0, keepdims=True)
        picks.append(jnp.where(slot_row == slot, 1.0, 0.0).astype(jnp.bfloat16))
        payloads.append(stresses[:, by].reshape(-1, LANES))
    chosen = jnp.concatenate(picks, axis=1)
    total = None
    for part in split_here(jnp.concatenate(payloads, axis=1)):
        sums = lax.dot_general(chosen, part, (((1,), (1,)), ((), ())), preferred_element_type=jnp.float32)
        total = sums if total is None else total + sums
    for d in range(outgoing.shape[0]):
        outgoing[d] = total[d * cap : (d + 1) * cap]


def call(kernel, out_shape, *args, scratch=(), hbm=0):
    whole = pl.BlockSpec(memory_space=pltpu.VMEM)
    held = [pltpu.with_memory_space_constraint(a, pltpu.VMEM if i >= hbm else pltpu.HBM) for i, a in enumerate(args)]
    return pl.pallas_call(
        kernel,
        out_shape=out_shape,
        in_specs=[pl.BlockSpec(memory_space=pltpu.HBM)] * hbm + [whole] * (len(args) - hbm),
        out_specs=jax.tree.map(lambda _: whole, out_shape),
        scratch_shapes=list(scratch),
        compiler_params=pltpu.CompilerParams(vmem_limit_bytes=VMEM_BYTES),
    )(*held)


def f32(*shape):
    return jax.ShapeDtypeStruct(shape, jnp.float32)


def per_device(fields, owner):
    _, _, height, width = fields.shape
    tiles = width // LANES
    rows = TERMS * LEVELS * ROWS
    lane_tile = (COMPONENTS, LEVELS, height, LANES)
    order = (0, tiles - 1) + tuple(range(1, tiles - 1))
    weights, third = [jnp.asarray(w) for w in split_weights(width, order)]
    rest = tiles - OUTER - READY
    message = f32(8, rows + 2 * EDGE)
    outer_inner, outer_edge, to_across, to_beside, ready = call(
        functools.partial(outer_kernel, order),
        (
            f32(OUTER, rows, LANES),
            f32(OUTER, 2 * EDGE, LANES),
            message,
            message,
            f32(READY, *lane_tile),
        ),
        fields,
        scratch=[
            pltpu.VMEM((OUTER, *lane_tile), jnp.float32),
            pltpu.SemaphoreType.DMA((OUTER, LEVELS)),
            pltpu.SemaphoreType.DMA((READY,)),
        ],
        hbm=1,
    )
    nx, ny = lax.axis_size("gx"), lax.axis_size("gy")
    beside_x = [(i, i ^ 1) for i in range(nx)]
    across_x = [(i, (i + 1) % nx if i % 2 else (i - 1) % nx) for i in range(nx)]
    up_y = [(i, (i + 1) % ny) for i in range(ny)]
    down_y = [(j, i) for i, j in up_y]
    across = lax.ppermute(to_across, "gx", across_x)
    beside = lax.ppermute(to_beside, "gx", beside_x)
    ready_inner, partial, later = call(
        functools.partial(middle_kernel, order),
        (f32(READY, rows, LANES), f32(2 * EDGE, LANES), f32(rest, *lane_tile)),
        fields,
        outer_edge,
        ready,
        weights,
        third,
        scratch=[pltpu.VMEM((READY + rest, 2 * EDGE, LANES), jnp.float32), pltpu.SemaphoreType.DMA((rest,))],
        hbm=1,
    )
    before, after = call(corner_kernel, (f32(EDGE, LANES), f32(EDGE, LANES)), partial, across, beside)
    from_south = lax.ppermute(after, "gy", up_y)
    from_north = lax.ppermute(before, "gy", down_y)
    coarse = call(
        coarse_kernel,
        f32(rows, LANES),
        outer_inner,
        ready_inner,
        later,
        weights,
        third,
        across,
        beside,
        scratch=[pltpu.VMEM((rest, rows, LANES), jnp.float32)],
    )
    devices = nx * ny
    blocks = owner.shape[0]
    cap = max(2, 2 * blocks // devices)
    pay = len(PRODUCT_PAIRS) * LEVELS * BLK * BLK
    outgoing = call(
        functools.partial(send_kernel, cap),
        f32(devices, cap, pay),
        coarse,
        from_south,
        from_north,
        owner.reshape(1, blocks),
        scratch=[pltpu.VMEM((rows, LANES), jnp.float32), pltpu.VMEM((pay * blocks * BLK // LANES, LANES), jnp.float32)],
    )
    arrived = lax.all_to_all(outgoing, ("gx", "gy"), split_axis=0, concat_axis=0, tiled=True)
    return arrived.reshape(devices * cap, pay)


def solution(mesh):
    placed = (P(None, None, "gy", "gx"), P(("gx", "gy"), None))
    return jax.shard_map(
        per_device, mesh=mesh, in_specs=placed, out_specs=P(("gx", "gy"), None), check_vma=False
    )
```

```python
import functools

import jax
import jax.numpy as jnp
import ml_dtypes
import numpy as np
from jax import lax
from jax.experimental import pallas as pl
from jax.experimental.pallas import tpu as pltpu
from jax.sharding import PartitionSpec as P

BLK = 4
RATIO = 10
LANES = 128
HIGHEST = lax.Precision.HIGHEST
SIGMA_CELLS = 2.8867513
PRODUCT_PAIRS = ((0, 0), (0, 1), (0, 2), (0, 3), (1, 1), (1, 2), (1, 3), (2, 2), (2, 3), (3, 3))
COMPONENTS = 4
TERMS = COMPONENTS + len(PRODUCT_PAIRS)
LEVELS = 4
ROWS = 8
OUTER = 2
BROUGHT = 4
FULL = 5
EDGE = TERMS * LEVELS
VMEM_BYTES = 16 * 1024 * 1024


def gauss_taps():
    spread = np.arange(21, dtype=np.float64) - 10.0
    values = np.exp(-spread * spread / (2.0 * SIGMA_CELLS * SIGMA_CELLS))
    return (values / values.sum()).astype(np.float32)


TAPS = gauss_taps()
G = [float(v) for v in TAPS]


def east_weights(columns):
    fine = np.arange(columns)[:, None]
    coarse = np.arange(columns // RATIO)[None, :]
    tap = fine - RATIO * coarse + 5
    inside = (tap >= 0) & (tap <= 20)
    return np.where(inside, TAPS[np.clip(tap, 0, 20)], np.float32(0))


def split(values):
    parts = []
    for _ in range(3):
        part = values.astype(ml_dtypes.bfloat16)
        parts.append(part)
        values = values - part.astype(np.float32)
    return parts


def split_weights(columns, order):
    tiles = east_weights(columns).reshape(-1, LANES, columns // RATIO)
    first, second, third = split(tiles[list(order)].reshape(columns, -1))
    return np.concatenate([first, second], axis=1), third


def beyond_weights():
    row = lax.broadcasted_iota(jnp.int32, (16, LANES), 0)
    lane = lax.broadcasted_iota(jnp.int32, (16, LANES), 1)
    weights = jnp.zeros((16, LANES), jnp.float32)
    for side, taps in ((0, enumerate(G[15:21])), (8, enumerate(G[0:5], LANES - 5))):
        for at, tap in taps:
            weights = jnp.where((row == side) & (lane == at), tap, weights)
    return weights


def edge_places():
    odd = lax.axis_index("gx") % 2
    row = lax.broadcasted_iota(jnp.int32, (ROWS, LANES), 0)
    lane = lax.broadcasted_iota(jnp.int32, (ROWS, LANES), 1)
    across = odd * (LANES - 1)
    return jnp.where((row == 0) & (lane == across) | (row == 1) & (lane == LANES - 1 - across), 1.0, 0.0)


def weighed(values, weight):
    scaled = [v * weight for v in values]
    return scaled + [scaled[a] * values[b] for a, b in PRODUCT_PAIRS]


def added(sums, terms):
    return [s + t for s, t in zip(sums, terms)]


def strided(tile, level, p):
    start = level * (tile.shape[1] // LEVELS) + p
    return [tile[c, pl.ds(start, ROWS, stride=RATIO), :] for c in range(COMPONENTS)]


def end_sums(tile, edge):
    height = tile.shape[1] // LEVELS
    row = lax.broadcasted_iota(jnp.int32, (ROWS, LANES), 0)
    total = None
    for p in range(6):
        ends = (pl.ds(p, LEVELS, stride=height), pl.ds(height - 6 + p, LEVELS, stride=height))
        values = [jnp.concatenate([tile[c, end, :] for end in ends], axis=0) for c in range(COMPONENTS)]
        terms = weighed(values, jnp.where(row < LEVELS, G[p + 15], G[p - 1] if p else 0.0))
        total = terms if total is None else added(total, terms)
    for q, value in enumerate(total):
        edge[pl.ds(q * ROWS, ROWS), :] = value


GROUPS = ((0, 1, 2, 3, 4, 5, 6, 7), (8, 9, 10, 11, 12, 13))


def filter_level(load, level, inner, edge=None):
    for group in GROUPS:

        def terms_of(p, weight):
            values = load(level, p)
            scaled = [v * weight for v in values]
            pairs = [PRODUCT_PAIRS[q - COMPONENTS] if q >= COMPONENTS else (q, None) for q in group]
            return [scaled[a] if b is None else scaled[a] * values[b] for a, b in pairs]

        own = below = terms_of(0, G[5])
        for p in range(1, 5):
            own = added(own, terms_of(p, G[p + 5]))
            below = added(below, terms_of(p, G[p + 15]))
        own = added(own, terms_of(5, G[10]))
        above = terms_of(5, G[0])
        below = added(below, above)
        if edge is not None:
            for q, value in zip(group, below):
                edge[pl.ds(q * ROWS + level, 1), :] = value[0:1]
        own = [o + pltpu.roll(v, ROWS - 1, 0) for o, v in zip(own, below)]
        for p in range(6, RATIO):
            own = added(own, terms_of(p, G[p + 5]))
            above = added(above, terms_of(p, G[p - 5]))
        for q, o, value in zip(group, own, above):
            inner[pl.ds((q * LEVELS + level) * ROWS, ROWS), :] = o + pltpu.roll(value, 1, 0)
            if edge is not None:
                edge[pl.ds(q * ROWS + LEVELS + level, 1), :] = value[ROWS - 1 : ROWS]


def tile_copies(fields, places, sems):
    return [
        pltpu.make_async_copy(fields.at[:, :, pl.ds(t * LANES, LANES)], place, sems.at[i])
        for i, (t, place) in enumerate(places)
    ]


def outer_kernel(order, fields, across, beside, ready, inner, edge, level_sems, sems):
    height = fields.shape[1] // LEVELS
    arriving = []
    for level in range(LEVELS):
        rows = pl.ds(level * height, height)
        arriving.append(
            [
                pltpu.make_async_copy(
                    fields.at[:, rows, pl.ds(order[i] * LANES, LANES)], ready.at[i, :, rows], level_sems.at[i, level]
                )
                for i in range(OUTER)
            ]
        )
    copies = tile_copies(fields, [(order[i], ready.at[i]) for i in range(OUTER, BROUGHT)], sems)
    for copy in sum(arriving, []) + copies:
        copy.start()
    lane = lax.broadcasted_iota(jnp.int32, (ROWS, LANES), 1)

    def merged(level, p):
        first, last = (strided(ready.at[i], level, p) for i in range(OUTER))
        return [jnp.where(lane < LANES // 2, f, s) for f, s in zip(first, last)]

    for level in range(LEVELS):
        for copy in arriving[level]:
            copy.wait()
        filter_level(merged, level, inner, edge)
    beyond = jnp.concatenate(split_here(beyond_weights()), axis=0)
    total = None
    for part in split_here(jnp.concatenate([inner[...], edge[...]], axis=0)):
        sums = lax.dot_general(beyond, part, (((1,), (1,)), ((), ())), preferred_element_type=jnp.float32)
        total = sums if total is None else total + sums
    messages = total[:16] + (total[16:32] + total[32:])
    odd = lax.axis_index("gx") % 2 == 1
    across[...] = jnp.where(odd, messages[8:9], messages[:1])
    beside[...] = jnp.where(odd, messages[:1], messages[8:9])
    for copy in copies:
        copy.wait()


def split_here(values):
    first = values.astype(jnp.bfloat16)
    left = values - first.astype(jnp.float32)
    second = left.astype(jnp.bfloat16)
    return first, second, (left - second.astype(jnp.float32)).astype(jnp.bfloat16)


def dot(a, b):
    return jnp.dot(a, b, preferred_element_type=jnp.float32)


def east_sums(values, pair, weights, third):
    rows = pl.ds(pair * 2 * LANES, 2 * LANES)
    a, b, c = split_here(values)
    both = dot(a, weights[rows, :]) + dot(b, weights[rows, :])
    small = dot(a, third[rows, :]) + dot(c, weights[rows, :LANES])
    return both[:, :LANES] + (both[:, LANES:] + small)


def middle_kernel(order, fields, ready, weights, third, inner, partial, later, tile, edge, sems):
    places = [tile.at[i] for i in range(FULL - BROUGHT)] + [later.at[i] for i in range(len(order) - FULL)]
    copies = tile_copies(fields, list(zip(order[BROUGHT:], places)), sems)
    for copy in copies:
        copy.start()
    tiles = [ready.at[i] for i in range(BROUGHT)] + places

    def add(pair):
        both = jnp.concatenate([edge[2 * pair], edge[2 * pair + 1]], axis=1)
        part = east_sums(both, pair, weights, third)
        partial[...] = part if pair == 0 else partial[...] + part

    for i in range(len(order)):
        if i >= BROUGHT:
            copies[i - BROUGHT].wait()
        if i < FULL:
            for level in range(LEVELS):
                filter_level(functools.partial(strided, tiles[i]), level, inner.at[i], edge.at[i])
        else:
            end_sums(tiles[i], edge.at[i])
    for pair in range(len(order) // 2):
        add(pair)


def from_sides(across, beside):
    none = jnp.zeros((ROWS - 2, across.shape[1]), jnp.float32)
    both = jnp.concatenate([across, beside, none], axis=0)
    return lax.dot_general(
        both, edge_places(), (((0,), (0,)), ((), ())), precision=HIGHEST, preferred_element_type=jnp.float32
    )


def corner_kernel(partial, across, beside, before, after):
    start = TERMS * LEVELS * ROWS
    total = partial[...] + from_sides(across[:, start:], beside[:, start:])
    for q in range(TERMS):
        rows = pl.ds(q * LEVELS, LEVELS)
        before[rows, :] = total[q * ROWS : q * ROWS + LEVELS]
        after[rows, :] = total[q * ROWS + LEVELS : (q + 1) * ROWS]


def coarse_kernel(full_inner, later, weights, third, across, beside, coarse, inner):
    count = later.shape[0]
    tiles = [full_inner.at[i] for i in range(FULL)] + [inner.at[i] for i in range(count)]
    stop = TERMS * LEVELS * ROWS
    coarse[...] = from_sides(across[:, :stop], beside[:, :stop])

    def add(pair):
        both = jnp.concatenate([tiles[2 * pair][...], tiles[2 * pair + 1][...]], axis=1)
        coarse[...] += east_sums(both, pair, weights, third)

    done = 0
    for i in range(count):
        if 2 * done + 2 <= FULL + i:
            add(done)
            done += 1
        for level in range(LEVELS):
            filter_level(functools.partial(strided, later.at[i]), level, inner.at[i])
    for pair in range(done, len(tiles) // 2):
        add(pair)


def send_kernel(cap, coarse, south, north, before, after, owner, outgoing, filtered, spread):
    filtered[...] = coarse[...]
    slab = LEVELS * ROWS
    filtered[pl.ds(0, EDGE, stride=ROWS), :] += south[...] - after[...]
    filtered[pl.ds(ROWS - 1, EDGE, stride=ROWS), :] += north[...] - before[...]
    means = [filtered[c * slab : (c + 1) * slab, :] for c in range(COMPONENTS)]
    lane = lax.broadcasted_iota(jnp.int32, (slab, LANES), 1) % BLK
    for k, (a, b) in enumerate(PRODUCT_PAIRS):
        q = COMPONENTS + k
        stress = filtered[q * slab : (q + 1) * slab, :] - means[a] * means[b]
        for c in range(BLK):
            spread[pl.ds(k * slab * BLK + c, slab, stride=BLK), :] = jnp.where(lane == c, stress, 0.0)
    slots = outgoing.shape[0] * outgoing.shape[1]
    blocks = owner.shape[1]
    across = LANES // BLK
    own = lax.broadcasted_iota(jnp.int32, (blocks, blocks), 0) == lax.broadcasted_iota(jnp.int32, (blocks, blocks), 1)
    column = jnp.sum(jnp.where(own, jnp.broadcast_to(owner[...], (blocks, blocks)), 0), axis=1, keepdims=True)
    index = lax.broadcasted_iota(jnp.int32, (blocks, LANES), 0)
    named = jnp.broadcast_to(column, (blocks, LANES))
    slot_row = lax.broadcasted_iota(jnp.int32, (slots, LANES), 0)
    stresses = spread[...].reshape(len(PRODUCT_PAIRS) * LEVELS, blocks // across, BLK * BLK, LANES)
    picks, payloads = [], []
    for by in range(blocks // across):
        block = by * across + lax.broadcasted_iota(jnp.int32, (blocks, LANES), 1) // BLK
        mine = jnp.sum(jnp.where(index == block, named, 0), axis=0, keepdims=True)
        earlier = jnp.where((index < block) & (named == mine), 1, 0)
        slot = mine * cap + jnp.sum(earlier, axis=0, keepdims=True)
        picks.append(jnp.where(slot_row == slot, 1.0, 0.0).astype(jnp.bfloat16))
        payloads.append(stresses[:, by].reshape(-1, LANES))
    chosen = jnp.concatenate(picks, axis=1)
    total = None
    for part in split_here(jnp.concatenate(payloads, axis=1)):
        sums = lax.dot_general(chosen, part, (((1,), (1,)), ((), ())), preferred_element_type=jnp.float32)
        total = sums if total is None else total + sums
    for d in range(outgoing.shape[0]):
        outgoing[d] = total[d * cap : (d + 1) * cap]


def call(kernel, out_shape, *args, scratch=(), hbm=0):
    whole = pl.BlockSpec(memory_space=pltpu.VMEM)
    held = [pltpu.with_memory_space_constraint(a, pltpu.VMEM if i >= hbm else pltpu.HBM) for i, a in enumerate(args)]
    return pl.pallas_call(
        kernel,
        out_shape=out_shape,
        in_specs=[pl.BlockSpec(memory_space=pltpu.HBM)] * hbm + [whole] * (len(args) - hbm),
        out_specs=jax.tree.map(lambda _: whole, out_shape),
        scratch_shapes=list(scratch),
        compiler_params=pltpu.CompilerParams(vmem_limit_bytes=VMEM_BYTES),
    )(*held)


def f32(*shape):
    return jax.ShapeDtypeStruct(shape, jnp.float32)


def per_device(fields, owner):
    _, _, height, width = fields.shape
    tiles = width // LANES
    rows = TERMS * LEVELS * ROWS
    flat = fields.reshape(COMPONENTS, LEVELS * height, width)
    lane_tile = (COMPONENTS, LEVELS * height, LANES)
    order = (0, tiles - 1) + tuple(range(1, tiles - 1))
    weights, third = [jnp.asarray(w) for w in split_weights(width, order)]
    rest = tiles - FULL
    message = f32(1, rows + 2 * EDGE)
    to_across, to_beside, ready = call(
        functools.partial(outer_kernel, order),
        (message, message, f32(BROUGHT, *lane_tile)),
        flat,
        scratch=[
            pltpu.VMEM((rows, LANES), jnp.float32),
            pltpu.VMEM((2 * EDGE, LANES), jnp.float32),
            pltpu.SemaphoreType.DMA((OUTER, LEVELS)),
            pltpu.SemaphoreType.DMA((BROUGHT - OUTER,)),
        ],
        hbm=1,
    )
    nx, ny = lax.axis_size("gx"), lax.axis_size("gy")
    beside_x = [(i, i ^ 1) for i in range(nx)]
    across_x = [(i, (i + 1) % nx if i % 2 else (i - 1) % nx) for i in range(nx)]
    up_y = [(i, (i + 1) % ny) for i in range(ny)]
    down_y = [(j, i) for i, j in up_y]
    across = lax.ppermute(to_across, "gx", across_x)
    beside = lax.ppermute(to_beside, "gx", beside_x)
    full_inner, partial, later = call(
        functools.partial(middle_kernel, order),
        (f32(FULL, rows, LANES), f32(2 * EDGE, LANES), f32(rest, *lane_tile)),
        flat,
        ready,
        weights,
        third,
        scratch=[
            pltpu.VMEM((FULL - BROUGHT, *lane_tile), jnp.float32),
            pltpu.VMEM((tiles, 2 * EDGE, LANES), jnp.float32),
            pltpu.SemaphoreType.DMA((tiles - BROUGHT,)),
        ],
        hbm=1,
    )
    before, after = call(corner_kernel, (f32(EDGE, LANES), f32(EDGE, LANES)), partial, across, beside)
    from_south = lax.ppermute(after, "gy", up_y)
    from_north = lax.ppermute(before, "gy", down_y)
    coarse = call(
        coarse_kernel,
        f32(rows, LANES),
        full_inner,
        later,
        weights,
        third,
        across,
        beside,
        scratch=[pltpu.VMEM((rest, rows, LANES), jnp.float32)],
    )
    devices = nx * ny
    blocks = owner.shape[0]
    cap = max(2, 2 * blocks // devices)
    pay = len(PRODUCT_PAIRS) * LEVELS * BLK * BLK
    outgoing = call(
        functools.partial(send_kernel, cap),
        f32(devices, cap, pay),
        coarse,
        from_south,
        from_north,
        before,
        after,
        owner.reshape(1, blocks),
        scratch=[pltpu.VMEM((rows, LANES), jnp.float32), pltpu.VMEM((pay * blocks * BLK // LANES, LANES), jnp.float32)],
    )
    arrived = lax.all_to_all(outgoing, ("gx", "gy"), split_axis=0, concat_axis=0, tiled=True)
    return arrived.reshape(devices * cap, pay)


def solution(mesh):
    placed = (P(None, None, "gy", "gx"), P(("gx", "gy"), None))
    return jax.shard_map(
        per_device, mesh=mesh, in_specs=placed, out_specs=P(("gx", "gy"), None), check_vma=False
    )
```

```python
import functools

import jax
import jax.numpy as jnp
import ml_dtypes
import numpy as np
from jax import lax
from jax.experimental import pallas as pl
from jax.experimental.pallas import tpu as pltpu
from jax.sharding import PartitionSpec as P

BLK = 4
RATIO = 10
LANES = 128
HIGHEST = lax.Precision.HIGHEST
SIGMA_CELLS = 2.8867513
PRODUCT_PAIRS = ((0, 0), (0, 1), (0, 2), (0, 3), (1, 1), (1, 2), (1, 3), (2, 2), (2, 3), (3, 3))
COMPONENTS = 4
TERMS = COMPONENTS + len(PRODUCT_PAIRS)
LEVELS = 4
ROWS = 8
OUTER = 2
BROUGHT = 4
FULL = 5
EDGE = TERMS * LEVELS
VMEM_BYTES = 16 * 1024 * 1024


def gauss_taps():
    spread = np.arange(21, dtype=np.float64) - 10.0
    values = np.exp(-spread * spread / (2.0 * SIGMA_CELLS * SIGMA_CELLS))
    return (values / values.sum()).astype(np.float32)


TAPS = gauss_taps()
G = [float(v) for v in TAPS]


def east_weights(columns):
    fine = np.arange(columns)[:, None]
    coarse = np.arange(columns // RATIO)[None, :]
    tap = fine - RATIO * coarse + 5
    inside = (tap >= 0) & (tap <= 20)
    return np.where(inside, TAPS[np.clip(tap, 0, 20)], np.float32(0))


def split(values):
    parts = []
    for _ in range(3):
        part = values.astype(ml_dtypes.bfloat16)
        parts.append(part)
        values = values - part.astype(np.float32)
    return parts


def split_weights(columns, order):
    tiles = east_weights(columns).reshape(-1, LANES, columns // RATIO)
    first, second, third = split(tiles[list(order)].reshape(columns, -1))
    return np.concatenate([first, second], axis=1), third


def beyond_weights():
    row = lax.broadcasted_iota(jnp.int32, (16, LANES), 0)
    lane = lax.broadcasted_iota(jnp.int32, (16, LANES), 1)
    weights = jnp.zeros((16, LANES), jnp.float32)
    for side, taps in ((0, enumerate(G[15:21])), (8, enumerate(G[0:5], LANES - 5))):
        for at, tap in taps:
            weights = jnp.where((row == side) & (lane == at), tap, weights)
    return weights


def edge_places():
    odd = lax.axis_index("gx") % 2
    row = lax.broadcasted_iota(jnp.int32, (ROWS, LANES), 0)
    lane = lax.broadcasted_iota(jnp.int32, (ROWS, LANES), 1)
    across = odd * (LANES - 1)
    return jnp.where((row == 0) & (lane == across) | (row == 1) & (lane == LANES - 1 - across), 1.0, 0.0)


def weighed(values, weight):
    scaled = [v * weight for v in values]
    return scaled + [scaled[a] * values[b] for a, b in PRODUCT_PAIRS]


def added(sums, terms):
    return [s + t for s, t in zip(sums, terms)]


def strided(tile, level, p):
    start = level * (tile.shape[1] // LEVELS) + p
    return [tile[c, pl.ds(start, ROWS, stride=RATIO), :] for c in range(COMPONENTS)]


def end_sums(tile, edge):
    height = tile.shape[1] // LEVELS
    row = lax.broadcasted_iota(jnp.int32, (ROWS, LANES), 0)
    total = None
    for p in range(6):
        ends = (pl.ds(p, LEVELS, stride=height), pl.ds(height - 6 + p, LEVELS, stride=height))
        values = [jnp.concatenate([tile[c, end, :] for end in ends], axis=0) for c in range(COMPONENTS)]
        terms = weighed(values, jnp.where(row < LEVELS, G[p + 15], G[p - 1] if p else 0.0))
        total = terms if total is None else added(total, terms)
    for q, value in enumerate(total):
        edge[pl.ds(q * ROWS, ROWS), :] = value


GROUPS = ((0, 1, 2, 3, 4, 5, 6, 7), (8, 9, 10, 11, 12, 13))


def filter_level(load, level, inner, edge=None):
    for group in GROUPS:

        def terms_of(p, weight):
            values = load(level, p)
            scaled = [v * weight for v in values]
            pairs = [PRODUCT_PAIRS[q - COMPONENTS] if q >= COMPONENTS else (q, None) for q in group]
            return [scaled[a] if b is None else scaled[a] * values[b] for a, b in pairs]

        own = below = terms_of(0, G[5])
        for p in range(1, 5):
            own = added(own, terms_of(p, G[p + 5]))
            below = added(below, terms_of(p, G[p + 15]))
        own = added(own, terms_of(5, G[10]))
        above = terms_of(5, G[0])
        below = added(below, above)
        if edge is not None:
            for q, value in zip(group, below):
                edge[pl.ds(q * ROWS + level, 1), :] = value[0:1]
        own = [o + pltpu.roll(v, ROWS - 1, 0) for o, v in zip(own, below)]
        for p in range(6, RATIO):
            own = added(own, terms_of(p, G[p + 5]))
            above = added(above, terms_of(p, G[p - 5]))
        for q, o, value in zip(group, own, above):
            inner[pl.ds((q * LEVELS + level) * ROWS, ROWS), :] = o + pltpu.roll(value, 1, 0)
            if edge is not None:
                edge[pl.ds(q * ROWS + LEVELS + level, 1), :] = value[ROWS - 1 : ROWS]


def tile_copies(fields, places, sems):
    return [
        pltpu.make_async_copy(fields.at[:, :, pl.ds(t * LANES, LANES)], place, sems.at[i])
        for i, (t, place) in enumerate(places)
    ]


def outer_kernel(order, fields, across, beside, ready, inner, edge, level_sems, sems):
    height = fields.shape[1] // LEVELS
    arriving = []
    for level in range(LEVELS):
        rows = pl.ds(level * height, height)
        arriving.append(
            [
                pltpu.make_async_copy(
                    fields.at[:, rows, pl.ds(order[i] * LANES, LANES)], ready.at[i, :, rows], level_sems.at[i, level]
                )
                for i in range(OUTER)
            ]
        )
    copies = tile_copies(fields, [(order[i], ready.at[i]) for i in range(OUTER, BROUGHT)], sems)
    for copy in sum(arriving, []) + copies:
        copy.start()
    lane = lax.broadcasted_iota(jnp.int32, (ROWS, LANES), 1)

    def merged(level, p):
        first, last = (strided(ready.at[i], level, p) for i in range(OUTER))
        return [jnp.where(lane < LANES // 2, f, s) for f, s in zip(first, last)]

    for level in range(LEVELS):
        for copy in arriving[level]:
            copy.wait()
        filter_level(merged, level, inner, edge)
    beyond = jnp.concatenate(split_here(beyond_weights()), axis=0)
    total = None
    for part in split_here(jnp.concatenate([inner[...], edge[...]], axis=0)):
        sums = lax.dot_general(beyond, part, (((1,), (1,)), ((), ())), preferred_element_type=jnp.float32)
        total = sums if total is None else total + sums
    messages = total[:16] + (total[16:32] + total[32:])
    odd = lax.axis_index("gx") % 2 == 1
    across[...] = jnp.where(odd, messages[8:9], messages[:1])
    beside[...] = jnp.where(odd, messages[:1], messages[8:9])
    for copy in copies:
        copy.wait()


def split_here(values):
    first = values.astype(jnp.bfloat16)
    left = values - first.astype(jnp.float32)
    second = left.astype(jnp.bfloat16)
    return first, second, (left - second.astype(jnp.float32)).astype(jnp.bfloat16)


def dot(a, b):
    return jnp.dot(a, b, preferred_element_type=jnp.float32)


def east_sums(values, pair, weights, third):
    rows = pl.ds(pair * 2 * LANES, 2 * LANES)
    a, b, c = split_here(values)
    both = dot(a, weights[rows, :]) + dot(b, weights[rows, :])
    small = dot(a, third[rows, :]) + dot(c, weights[rows, :LANES])
    return both[:, :LANES] + (both[:, LANES:] + small)


def middle_kernel(order, fields, ready, weights, third, inner, partial, later, tile, edge, sems):
    places = [tile.at[i] for i in range(FULL - BROUGHT)] + [later.at[i] for i in range(len(order) - FULL)]
    copies = tile_copies(fields, list(zip(order[BROUGHT:], places)), sems)
    for copy in copies:
        copy.start()
    tiles = [ready.at[i] for i in range(BROUGHT)] + places

    def add(pair):
        both = jnp.concatenate([edge[2 * pair], edge[2 * pair + 1]], axis=1)
        part = east_sums(both, pair, weights, third)
        partial[...] = part if pair == 0 else partial[...] + part

    for i in range(len(order)):
        if i >= BROUGHT:
            copies[i - BROUGHT].wait()
        if i < FULL:
            for level in range(LEVELS):
                filter_level(functools.partial(strided, tiles[i]), level, inner.at[i], edge.at[i])
        else:
            end_sums(tiles[i], edge.at[i])
    for pair in range(len(order) // 2):
        add(pair)


def from_sides(across, beside):
    none = jnp.zeros((ROWS - 2, across.shape[1]), jnp.float32)
    both = jnp.concatenate([across, beside, none], axis=0)
    return lax.dot_general(
        both, edge_places(), (((0,), (0,)), ((), ())), precision=HIGHEST, preferred_element_type=jnp.float32
    )


def corner_kernel(partial, across, beside, before, after):
    start = TERMS * LEVELS * ROWS
    total = partial[...] + from_sides(across[:, start:], beside[:, start:])
    for q in range(TERMS):
        rows = pl.ds(q * LEVELS, LEVELS)
        before[rows, :] = total[q * ROWS : q * ROWS + LEVELS]
        after[rows, :] = total[q * ROWS + LEVELS : (q + 1) * ROWS]


def coarse_kernel(full_inner, later, weights, third, across, beside, coarse, inner):
    count = later.shape[0]
    tiles = [full_inner.at[i] for i in range(FULL)] + [inner.at[i] for i in range(count)]
    stop = TERMS * LEVELS * ROWS
    coarse[...] = from_sides(across[:, :stop], beside[:, :stop])

    def add(pair):
        both = jnp.concatenate([tiles[2 * pair][...], tiles[2 * pair + 1][...]], axis=1)
        coarse[...] += east_sums(both, pair, weights, third)

    done = 0
    for i in range(count):
        if 2 * done + 2 <= FULL + i:
            add(done)
            done += 1
        for level in range(LEVELS):
            filter_level(functools.partial(strided, later.at[i]), level, inner.at[i])
    for pair in range(done, len(tiles) // 2):
        add(pair)


def send_kernel(cap, coarse, south, north, before, after, owner, outgoing, filtered, spread):
    filtered[...] = coarse[...]
    slab = LEVELS * ROWS
    filtered[pl.ds(0, EDGE, stride=ROWS), :] += south[...] - after[...]
    filtered[pl.ds(ROWS - 1, EDGE, stride=ROWS), :] += north[...] - before[...]
    means = [filtered[c * slab : (c + 1) * slab, :] for c in range(COMPONENTS)]
    lane = lax.broadcasted_iota(jnp.int32, (slab, LANES), 1) % BLK
    for k, (a, b) in enumerate(PRODUCT_PAIRS):
        q = COMPONENTS + k
        stress = filtered[q * slab : (q + 1) * slab, :] - means[a] * means[b]
        for c in range(BLK):
            spread[pl.ds(k * slab * BLK + c, slab, stride=BLK), :] = jnp.where(lane == c, stress, 0.0)
    slots = outgoing.shape[0] * outgoing.shape[1]
    blocks = owner.shape[1]
    across = LANES // BLK
    own = lax.broadcasted_iota(jnp.int32, (blocks, blocks), 0) == lax.broadcasted_iota(jnp.int32, (blocks, blocks), 1)
    column = jnp.sum(jnp.where(own, jnp.broadcast_to(owner[...], (blocks, blocks)), 0), axis=1, keepdims=True)
    index = lax.broadcasted_iota(jnp.int32, (blocks, LANES), 0)
    named = jnp.broadcast_to(column, (blocks, LANES))
    slot_row = lax.broadcasted_iota(jnp.int32, (slots, LANES), 0)
    stresses = spread[...].reshape(len(PRODUCT_PAIRS) * LEVELS, blocks // across, BLK * BLK, LANES)
    picks, payloads = [], []
    for by in range(blocks // across):
        block = by * across + lax.broadcasted_iota(jnp.int32, (blocks, LANES), 1) // BLK
        mine = jnp.sum(jnp.where(index == block, named, 0), axis=0, keepdims=True)
        earlier = jnp.where((index < block) & (named == mine), 1, 0)
        slot = mine * cap + jnp.sum(earlier, axis=0, keepdims=True)
        picks.append(jnp.where(slot_row == slot, 1.0, 0.0).astype(jnp.bfloat16))
        payloads.append(stresses[:, by].reshape(-1, LANES))
    chosen = jnp.concatenate(picks, axis=1)
    total = None
    for part in split_here(jnp.concatenate(payloads, axis=1)):
        sums = lax.dot_general(chosen, part, (((1,), (1,)), ((), ())), preferred_element_type=jnp.float32)
        total = sums if total is None else total + sums
    for d in range(outgoing.shape[0]):
        outgoing[d] = total[d * cap : (d + 1) * cap]


def place_kernel(arrived, received, rows, sems):
    parts = rows.shape[0]
    sources, cap, _ = arrived.shape
    count = sources // parts
    copies = []
    for part in range(parts):
        for d in range(count):
            rows[part, pl.ds(d * cap, cap), :] = arrived[part * count + d]
        copies.append(
            pltpu.make_async_copy(
                rows.at[part], received.at[pl.ds(part * count * cap, count * cap), :], sems.at[part]
            )
        )
        copies[-1].start()
    for copy in copies:
        copy.wait()


def call(kernel, out_shape, *args, scratch=(), hbm=0, out=pltpu.VMEM):
    whole = pl.BlockSpec(memory_space=pltpu.VMEM)
    held = [pltpu.with_memory_space_constraint(a, pltpu.VMEM if i >= hbm else pltpu.HBM) for i, a in enumerate(args)]
    return pl.pallas_call(
        kernel,
        out_shape=out_shape,
        in_specs=[pl.BlockSpec(memory_space=pltpu.HBM)] * hbm + [whole] * (len(args) - hbm),
        out_specs=jax.tree.map(lambda _: pl.BlockSpec(memory_space=out), out_shape),
        scratch_shapes=list(scratch),
        compiler_params=pltpu.CompilerParams(vmem_limit_bytes=VMEM_BYTES),
    )(*held)


def f32(*shape):
    return jax.ShapeDtypeStruct(shape, jnp.float32)


def per_device(fields, owner):
    _, _, height, width = fields.shape
    tiles = width // LANES
    rows = TERMS * LEVELS * ROWS
    flat = fields.reshape(COMPONENTS, LEVELS * height, width)
    lane_tile = (COMPONENTS, LEVELS * height, LANES)
    order = (0, tiles - 1) + tuple(range(1, tiles - 1))
    weights, third = [jnp.asarray(w) for w in split_weights(width, order)]
    rest = tiles - FULL
    message = f32(1, rows + 2 * EDGE)
    to_across, to_beside, ready = call(
        functools.partial(outer_kernel, order),
        (message, message, f32(BROUGHT, *lane_tile)),
        flat,
        scratch=[
            pltpu.VMEM((rows, LANES), jnp.float32),
            pltpu.VMEM((2 * EDGE, LANES), jnp.float32),
            pltpu.SemaphoreType.DMA((OUTER, LEVELS)),
            pltpu.SemaphoreType.DMA((BROUGHT - OUTER,)),
        ],
        hbm=1,
    )
    nx, ny = lax.axis_size("gx"), lax.axis_size("gy")
    beside_x = [(i, i ^ 1) for i in range(nx)]
    across_x = [(i, (i + 1) % nx if i % 2 else (i - 1) % nx) for i in range(nx)]
    up_y = [(i, (i + 1) % ny) for i in range(ny)]
    down_y = [(j, i) for i, j in up_y]
    across = lax.ppermute(to_across, "gx", across_x)
    beside = lax.ppermute(to_beside, "gx", beside_x)
    full_inner, partial, later = call(
        functools.partial(middle_kernel, order),
        (f32(FULL, rows, LANES), f32(2 * EDGE, LANES), f32(rest, *lane_tile)),
        flat,
        ready,
        weights,
        third,
        scratch=[
            pltpu.VMEM((FULL - BROUGHT, *lane_tile), jnp.float32),
            pltpu.VMEM((tiles, 2 * EDGE, LANES), jnp.float32),
            pltpu.SemaphoreType.DMA((tiles - BROUGHT,)),
        ],
        hbm=1,
    )
    before, after = call(corner_kernel, (f32(EDGE, LANES), f32(EDGE, LANES)), partial, across, beside)
    from_south = lax.ppermute(after, "gy", up_y)
    from_north = lax.ppermute(before, "gy", down_y)
    coarse = call(
        coarse_kernel,
        f32(rows, LANES),
        full_inner,
        later,
        weights,
        third,
        across,
        beside,
        scratch=[pltpu.VMEM((rest, rows, LANES), jnp.float32)],
    )
    devices = nx * ny
    blocks = owner.shape[0]
    cap = max(2, 2 * blocks // devices)
    pay = len(PRODUCT_PAIRS) * LEVELS * BLK * BLK
    outgoing = call(
        functools.partial(send_kernel, cap),
        f32(devices, cap, pay),
        coarse,
        from_south,
        from_north,
        before,
        after,
        owner.reshape(1, blocks),
        scratch=[pltpu.VMEM((rows, LANES), jnp.float32), pltpu.VMEM((pay * blocks * BLK // LANES, LANES), jnp.float32)],
    )
    arrived = lax.all_to_all(outgoing, ("gx", "gy"), split_axis=0, concat_axis=0, tiled=True)
    parts = 4
    return call(
        place_kernel,
        f32(devices * cap, pay),
        arrived,
        scratch=[pltpu.VMEM((parts, devices * cap // parts, pay), jnp.float32), pltpu.SemaphoreType.DMA((parts,))],
        out=pltpu.HBM,
    )


def solution(mesh):
    placed = (P(None, None, "gy", "gx"), P(("gx", "gy"), None))
    return jax.shard_map(
        per_device, mesh=mesh, in_specs=placed, out_specs=P(("gx", "gy"), None), check_vma=False
    )
```

```python
import functools

import jax
import jax.numpy as jnp
import ml_dtypes
import numpy as np
from jax import lax
from jax.experimental import pallas as pl
from jax.experimental.pallas import tpu as pltpu
from jax.sharding import PartitionSpec as P

BLK = 4
RATIO = 10
LANES = 128
HIGHEST = lax.Precision.HIGHEST
SIGMA_CELLS = 2.8867513
PRODUCT_PAIRS = ((0, 0), (0, 1), (0, 2), (0, 3), (1, 1), (1, 2), (1, 3), (2, 2), (2, 3), (3, 3))
COMPONENTS = 4
TERMS = COMPONENTS + len(PRODUCT_PAIRS)
LEVELS = 4
ROWS = 8
OUTER = 2
BROUGHT = 4
FULL = 5
EDGE = TERMS * LEVELS
VMEM_BYTES = 16 * 1024 * 1024


def gauss_taps():
    spread = np.arange(21, dtype=np.float64) - 10.0
    values = np.exp(-spread * spread / (2.0 * SIGMA_CELLS * SIGMA_CELLS))
    return (values / values.sum()).astype(np.float32)


def two_parts(value):
    first = np.float64(ml_dtypes.bfloat16(value))
    return first + np.float64(ml_dtypes.bfloat16(value - first))


def rounded_taps(taps):
    taps = taps.astype(np.float64)
    taps, rounded = taps / taps.sum(), np.zeros(21)
    rounded[10] = two_parts(taps[10])
    left = taps[10] - rounded[10]
    for t in range(9, -1, -1):
        rounded[t] = rounded[20 - t] = two_parts(taps[t] + left / 2)
        left += 2 * (taps[t] - rounded[t])
    return rounded.astype(np.float32)


TAPS = gauss_taps()
G = [float(v) for v in TAPS]
EAST = rounded_taps(TAPS)


def east_weights(columns):
    fine = np.arange(columns)[:, None]
    coarse = np.arange(columns // RATIO)[None, :]
    tap = fine - RATIO * coarse + 5
    inside = (tap >= 0) & (tap <= 20)
    return np.where(inside, EAST[np.clip(tap, 0, 20)], np.float32(0))


def split_weights(columns, order):
    tiles = east_weights(columns).reshape(-1, LANES, columns // RATIO)
    weights = tiles[list(order)].reshape(columns, -1)
    first = weights.astype(ml_dtypes.bfloat16)
    return np.concatenate([first, (weights - first.astype(np.float32)).astype(ml_dtypes.bfloat16)], axis=1)


def beyond_weights():
    row = lax.broadcasted_iota(jnp.int32, (16, LANES), 0)
    lane = lax.broadcasted_iota(jnp.int32, (16, LANES), 1)
    weights = jnp.zeros((16, LANES), jnp.float32)
    for side, taps in ((0, enumerate(EAST[15:21])), (8, enumerate(EAST[:5], LANES - 5))):
        for at, tap in taps:
            weights = jnp.where((row == side) & (lane == at), float(tap), weights)
    return weights


def edge_places():
    odd = lax.axis_index("gx") % 2
    row = lax.broadcasted_iota(jnp.int32, (ROWS, LANES), 0)
    lane = lax.broadcasted_iota(jnp.int32, (ROWS, LANES), 1)
    across = odd * (LANES - 1)
    return jnp.where((row == 0) & (lane == across) | (row == 1) & (lane == LANES - 1 - across), 1.0, 0.0)


def weighed(values, weight):
    scaled = [v * weight for v in values]
    return scaled + [scaled[a] * values[b] for a, b in PRODUCT_PAIRS]


def added(sums, terms):
    return [s + t for s, t in zip(sums, terms)]


def strided(tile, level, p):
    start = level * (tile.shape[1] // LEVELS) + p
    return [tile[c, pl.ds(start, ROWS, stride=RATIO), :] for c in range(COMPONENTS)]


def end_sums(tile, edge):
    height = tile.shape[1] // LEVELS
    row = lax.broadcasted_iota(jnp.int32, (ROWS, LANES), 0)
    total = None
    for p in range(6):
        ends = (pl.ds(p, LEVELS, stride=height), pl.ds(height - 6 + p, LEVELS, stride=height))
        values = [jnp.concatenate([tile[c, end, :] for end in ends], axis=0) for c in range(COMPONENTS)]
        terms = weighed(values, jnp.where(row < LEVELS, G[p + 15], G[p - 1] if p else 0.0))
        total = terms if total is None else added(total, terms)
    for q, value in enumerate(total):
        edge[pl.ds(q * ROWS, ROWS), :] = value


GROUPS = ((0, 1, 2, 3, 4, 5, 6, 7), (8, 9, 10, 11, 12, 13))


def filter_level(load, level, inner, edge=None):
    for group in GROUPS:

        def terms_of(p, weight):
            values = load(level, p)
            scaled = [v * weight for v in values]
            pairs = [PRODUCT_PAIRS[q - COMPONENTS] if q >= COMPONENTS else (q, None) for q in group]
            return [scaled[a] if b is None else scaled[a] * values[b] for a, b in pairs]

        own = below = terms_of(0, G[5])
        for p in range(1, 5):
            own = added(own, terms_of(p, G[p + 5]))
            below = added(below, terms_of(p, G[p + 15]))
        own = added(own, terms_of(5, G[10]))
        above = terms_of(5, G[0])
        below = added(below, above)
        if edge is not None:
            for q, value in zip(group, below):
                edge[pl.ds(q * ROWS + level, 1), :] = value[0:1]
        own = [o + pltpu.roll(v, ROWS - 1, 0) for o, v in zip(own, below)]
        for p in range(6, RATIO):
            own = added(own, terms_of(p, G[p + 5]))
            above = added(above, terms_of(p, G[p - 5]))
        for q, o, value in zip(group, own, above):
            inner[pl.ds((q * LEVELS + level) * ROWS, ROWS), :] = o + pltpu.roll(value, 1, 0)
            if edge is not None:
                edge[pl.ds(q * ROWS + LEVELS + level, 1), :] = value[ROWS - 1 : ROWS]


def tile_copies(fields, places, sems):
    return [
        pltpu.make_async_copy(fields.at[:, :, pl.ds(t * LANES, LANES)], place, sems.at[i])
        for i, (t, place) in enumerate(places)
    ]


def outer_kernel(order, fields, across, beside, ready, inner, edge, level_sems, sems):
    height = fields.shape[1] // LEVELS
    arriving = []
    for level in range(LEVELS):
        rows = pl.ds(level * height, height)
        arriving.append(
            [
                pltpu.make_async_copy(
                    fields.at[:, rows, pl.ds(order[i] * LANES, LANES)], ready.at[i, :, rows], level_sems.at[i, level]
                )
                for i in range(OUTER)
            ]
        )
    copies = tile_copies(fields, [(order[i], ready.at[i]) for i in range(OUTER, BROUGHT)], sems)
    for copy in sum(arriving, []) + copies:
        copy.start()
    lane = lax.broadcasted_iota(jnp.int32, (ROWS, LANES), 1)

    def merged(level, p):
        first, last = (strided(ready.at[i], level, p) for i in range(OUTER))
        return [jnp.where(lane < LANES // 2, f, s) for f, s in zip(first, last)]

    for level in range(LEVELS):
        for copy in arriving[level]:
            copy.wait()
        filter_level(merged, level, inner, edge)
    beyond = jnp.concatenate(split_here(beyond_weights()), axis=0)
    total = None
    for part in split_here(jnp.concatenate([inner[...], edge[...]], axis=0)):
        sums = lax.dot_general(beyond, part, (((1,), (1,)), ((), ())), preferred_element_type=jnp.float32)
        total = sums if total is None else total + sums
    messages = total[:16] + (total[16:32] + total[32:])
    odd = lax.axis_index("gx") % 2 == 1
    across[...] = jnp.where(odd, messages[8:9], messages[:1])
    beside[...] = jnp.where(odd, messages[:1], messages[8:9])
    for copy in copies:
        copy.wait()


def split_here(values):
    first = values.astype(jnp.bfloat16)
    left = values - first.astype(jnp.float32)
    second = left.astype(jnp.bfloat16)
    return first, second, (left - second.astype(jnp.float32)).astype(jnp.bfloat16)


def dot(a, b):
    return jnp.dot(a, b, preferred_element_type=jnp.float32)


def east_sums(values, pair, weights):
    rows = pl.ds(pair * 2 * LANES, 2 * LANES)
    a, b, c = split_here(values)
    both = dot(a, weights[rows, :]) + dot(b, weights[rows, :])
    return both[:, :LANES] + (both[:, LANES:] + dot(c, weights[rows, :LANES]))


def east_sums_stacked(values, pair, weights):
    parts = dot(jnp.concatenate(split_here(values), axis=0), weights[pl.ds(pair * 2 * LANES, 2 * LANES), :])
    count = values.shape[0]
    sums = parts[:count] + (parts[count : 2 * count] + parts[2 * count :])
    return sums[:, :LANES] + sums[:, LANES:]


def middle_kernel(order, fields, ready, weights, inner, partial, later, tile, edge, sems):
    places = [tile.at[i] for i in range(FULL - BROUGHT)] + [later.at[i] for i in range(len(order) - FULL)]
    copies = tile_copies(fields, list(zip(order[BROUGHT:], places)), sems)
    for copy in copies:
        copy.start()
    tiles = [ready.at[i] for i in range(BROUGHT)] + places

    def add(pair):
        both = jnp.concatenate([edge[2 * pair], edge[2 * pair + 1]], axis=1)
        part = east_sums(both, pair, weights)
        partial[...] = part if pair == 0 else partial[...] + part

    for i in range(len(order)):
        if i >= BROUGHT:
            copies[i - BROUGHT].wait()
        if i < FULL:
            for level in range(LEVELS):
                filter_level(functools.partial(strided, tiles[i]), level, inner.at[i], edge.at[i])
        else:
            end_sums(tiles[i], edge.at[i])
    for pair in range(len(order) // 2):
        add(pair)


def from_sides(across, beside):
    none = jnp.zeros((ROWS - 2, across.shape[1]), jnp.float32)
    both = jnp.concatenate([across, beside, none], axis=0)
    return lax.dot_general(
        both, edge_places(), (((0,), (0,)), ((), ())), precision=HIGHEST, preferred_element_type=jnp.float32
    )


def corner_kernel(partial, across, beside, before, after):
    start = TERMS * LEVELS * ROWS
    total = partial[...] + from_sides(across[:, start:], beside[:, start:])
    for q in range(TERMS):
        rows = pl.ds(q * LEVELS, LEVELS)
        before[rows, :] = total[q * ROWS : q * ROWS + LEVELS]
        after[rows, :] = total[q * ROWS + LEVELS : (q + 1) * ROWS]


def coarse_kernel(full_inner, later, weights, across, beside, coarse, inner):
    count = later.shape[0]
    tiles = [full_inner.at[i] for i in range(FULL)] + [inner.at[i] for i in range(count)]
    stop = TERMS * LEVELS * ROWS
    coarse[...] = from_sides(across[:, :stop], beside[:, :stop])

    def add(pair):
        both = jnp.concatenate([tiles[2 * pair][...], tiles[2 * pair + 1][...]], axis=1)
        coarse[...] += east_sums(both, pair, weights)

    done = 0
    for i in range(count):
        if 2 * done + 2 <= FULL + i:
            add(done)
            done += 1
        for level in range(LEVELS):
            filter_level(functools.partial(strided, later.at[i]), level, inner.at[i])
    for pair in range(done, len(tiles) // 2):
        add(pair)


def send_kernel(cap, coarse, south, north, before, after, owner, outgoing, filtered, spread):
    filtered[...] = coarse[...]
    slab = LEVELS * ROWS
    filtered[pl.ds(0, EDGE, stride=ROWS), :] += south[...] - after[...]
    filtered[pl.ds(ROWS - 1, EDGE, stride=ROWS), :] += north[...] - before[...]
    means = [filtered[c * slab : (c + 1) * slab, :] for c in range(COMPONENTS)]
    lane = lax.broadcasted_iota(jnp.int32, (slab, LANES), 1) % BLK
    for k, (a, b) in enumerate(PRODUCT_PAIRS):
        q = COMPONENTS + k
        stress = filtered[q * slab : (q + 1) * slab, :] - means[a] * means[b]
        for c in range(BLK):
            spread[pl.ds(k * slab * BLK + c, slab, stride=BLK), :] = jnp.where(lane == c, stress, 0.0)
    slots = outgoing.shape[0] * outgoing.shape[1]
    blocks = owner.shape[1]
    across = LANES // BLK
    own = lax.broadcasted_iota(jnp.int32, (blocks, blocks), 0) == lax.broadcasted_iota(jnp.int32, (blocks, blocks), 1)
    column = jnp.sum(jnp.where(own, jnp.broadcast_to(owner[...], (blocks, blocks)), 0), axis=1, keepdims=True)
    index = lax.broadcasted_iota(jnp.int32, (blocks, LANES), 0)
    named = jnp.broadcast_to(column, (blocks, LANES))
    slot_row = lax.broadcasted_iota(jnp.int32, (slots, LANES), 0)
    stresses = spread[...].reshape(len(PRODUCT_PAIRS) * LEVELS, blocks // across, BLK * BLK, LANES)
    picks, payloads = [], []
    for by in range(blocks // across):
        block = by * across + lax.broadcasted_iota(jnp.int32, (blocks, LANES), 1) // BLK
        mine = jnp.sum(jnp.where(index == block, named, 0), axis=0, keepdims=True)
        earlier = jnp.where((index < block) & (named == mine), 1, 0)
        slot = mine * cap + jnp.sum(earlier, axis=0, keepdims=True)
        picks.append(jnp.where(slot_row == slot, 1.0, 0.0).astype(jnp.bfloat16))
        payloads.append(stresses[:, by].reshape(-1, LANES))
    chosen = jnp.concatenate(picks, axis=1)
    total = None
    for part in split_here(jnp.concatenate(payloads, axis=1)):
        sums = lax.dot_general(chosen, part, (((1,), (1,)), ((), ())), preferred_element_type=jnp.float32)
        total = sums if total is None else total + sums
    for d in range(outgoing.shape[0]):
        outgoing[d] = total[d * cap : (d + 1) * cap]


def place_kernel(arrived, received, rows, sems):
    parts = rows.shape[0]
    sources, cap, _ = arrived.shape
    count = sources // parts
    copies = []
    for part in range(parts):
        for d in range(count):
            rows[part, pl.ds(d * cap, cap), :] = arrived[part * count + d]
        copies.append(
            pltpu.make_async_copy(
                rows.at[part], received.at[pl.ds(part * count * cap, count * cap), :], sems.at[part]
            )
        )
        copies[-1].start()
    for copy in copies:
        copy.wait()


def call(kernel, out_shape, *args, scratch=(), hbm=0, out=pltpu.VMEM):
    whole = pl.BlockSpec(memory_space=pltpu.VMEM)
    held = [pltpu.with_memory_space_constraint(a, pltpu.VMEM if i >= hbm else pltpu.HBM) for i, a in enumerate(args)]
    return pl.pallas_call(
        kernel,
        out_shape=out_shape,
        in_specs=[pl.BlockSpec(memory_space=pltpu.HBM)] * hbm + [whole] * (len(args) - hbm),
        out_specs=jax.tree.map(lambda _: pl.BlockSpec(memory_space=out), out_shape),
        scratch_shapes=list(scratch),
        compiler_params=pltpu.CompilerParams(vmem_limit_bytes=VMEM_BYTES),
    )(*held)


def f32(*shape):
    return jax.ShapeDtypeStruct(shape, jnp.float32)


def per_device(fields, owner):
    _, _, height, width = fields.shape
    tiles = width // LANES
    rows = TERMS * LEVELS * ROWS
    flat = fields.reshape(COMPONENTS, LEVELS * height, width)
    lane_tile = (COMPONENTS, LEVELS * height, LANES)
    order = (0, tiles - 1) + tuple(range(1, tiles - 1))
    weights = jnp.asarray(split_weights(width, order))
    rest = tiles - FULL
    message = f32(1, rows + 2 * EDGE)
    to_across, to_beside, ready = call(
        functools.partial(outer_kernel, order),
        (message, message, f32(BROUGHT, *lane_tile)),
        flat,
        scratch=[
            pltpu.VMEM((rows, LANES), jnp.float32),
            pltpu.VMEM((2 * EDGE, LANES), jnp.float32),
            pltpu.SemaphoreType.DMA((OUTER, LEVELS)),
            pltpu.SemaphoreType.DMA((BROUGHT - OUTER,)),
        ],
        hbm=1,
    )
    nx, ny = lax.axis_size("gx"), lax.axis_size("gy")
    beside_x = [(i, i ^ 1) for i in range(nx)]
    across_x = [(i, (i + 1) % nx if i % 2 else (i - 1) % nx) for i in range(nx)]
    up_y = [(i, (i + 1) % ny) for i in range(ny)]
    down_y = [(j, i) for i, j in up_y]
    across = lax.ppermute(to_across, "gx", across_x)
    beside = lax.ppermute(to_beside, "gx", beside_x)
    full_inner, partial, later = call(
        functools.partial(middle_kernel, order),
        (f32(FULL, rows, LANES), f32(2 * EDGE, LANES), f32(rest, *lane_tile)),
        flat,
        ready,
        weights,
        scratch=[
            pltpu.VMEM((FULL - BROUGHT, *lane_tile), jnp.float32),
            pltpu.VMEM((tiles, 2 * EDGE, LANES), jnp.float32),
            pltpu.SemaphoreType.DMA((tiles - BROUGHT,)),
        ],
        hbm=1,
    )
    before, after = call(corner_kernel, (f32(EDGE, LANES), f32(EDGE, LANES)), partial, across, beside)
    from_south = lax.ppermute(after, "gy", up_y)
    from_north = lax.ppermute(before, "gy", down_y)
    coarse = call(
        coarse_kernel,
        f32(rows, LANES),
        full_inner,
        later,
        weights,
        across,
        beside,
        scratch=[pltpu.VMEM((rest, rows, LANES), jnp.float32)],
    )
    devices = nx * ny
    blocks = owner.shape[0]
    cap = max(2, 2 * blocks // devices)
    pay = len(PRODUCT_PAIRS) * LEVELS * BLK * BLK
    outgoing = call(
        functools.partial(send_kernel, cap),
        f32(devices, cap, pay),
        coarse,
        from_south,
        from_north,
        before,
        after,
        owner.reshape(1, blocks),
        scratch=[pltpu.VMEM((rows, LANES), jnp.float32), pltpu.VMEM((pay * blocks * BLK // LANES, LANES), jnp.float32)],
    )
    arrived = lax.all_to_all(outgoing, ("gx", "gy"), split_axis=0, concat_axis=0, tiled=True)
    parts = 4
    return call(
        place_kernel,
        f32(devices * cap, pay),
        arrived,
        scratch=[pltpu.VMEM((parts, devices * cap // parts, pay), jnp.float32), pltpu.SemaphoreType.DMA((parts,))],
        out=pltpu.HBM,
    )


def solution(mesh):
    placed = (P(None, None, "gy", "gx"), P(("gx", "gy"), None))
    return jax.shard_map(
        per_device, mesh=mesh, in_specs=placed, out_specs=P(("gx", "gy"), None), check_vma=False
    )
```

```python
import functools

import jax
import jax.numpy as jnp
import ml_dtypes
import numpy as np
from jax import lax
from jax.experimental import pallas as pl
from jax.experimental.pallas import tpu as pltpu
from jax.sharding import PartitionSpec as P

BLK = 4
RATIO = 10
LANES = 128
HIGHEST = lax.Precision.HIGHEST
SIGMA_CELLS = 2.8867513
PRODUCT_PAIRS = ((0, 0), (0, 1), (0, 2), (0, 3), (1, 1), (1, 2), (1, 3), (2, 2), (2, 3), (3, 3))
COMPONENTS = 4
TERMS = COMPONENTS + len(PRODUCT_PAIRS)
LEVELS = 4
ROWS = 8
OUTER = 2
BROUGHT = 4
FULL = 5
EDGE = TERMS * LEVELS
VMEM_BYTES = 16 * 1024 * 1024


def gauss_taps():
    spread = np.arange(21, dtype=np.float64) - 10.0
    values = np.exp(-spread * spread / (2.0 * SIGMA_CELLS * SIGMA_CELLS))
    return (values / values.sum()).astype(np.float32)


def two_parts(value):
    first = np.float64(ml_dtypes.bfloat16(value))
    return first + np.float64(ml_dtypes.bfloat16(value - first))


def rounded_taps(taps):
    taps = taps.astype(np.float64)
    taps, rounded = taps / taps.sum(), np.zeros(21)
    rounded[10] = two_parts(taps[10])
    left = taps[10] - rounded[10]
    for t in range(9, -1, -1):
        rounded[t] = rounded[20 - t] = two_parts(taps[t] + left / 2)
        left += 2 * (taps[t] - rounded[t])
    return rounded.astype(np.float32)


TAPS = gauss_taps()
G = [float(v) for v in TAPS]
EAST = rounded_taps(TAPS)


def east_weights(columns):
    fine = np.arange(columns)[:, None]
    coarse = np.arange(columns // RATIO)[None, :]
    tap = fine - RATIO * coarse + 5
    inside = (tap >= 0) & (tap <= 20)
    return np.where(inside, EAST[np.clip(tap, 0, 20)], np.float32(0))


def split_weights(columns, order):
    tiles = east_weights(columns).reshape(-1, LANES, columns // RATIO)
    weights = tiles[list(order)].reshape(columns, -1)
    first = weights.astype(ml_dtypes.bfloat16)
    return np.concatenate([first, (weights - first.astype(np.float32)).astype(ml_dtypes.bfloat16)], axis=1)


def beyond_weights():
    row = lax.broadcasted_iota(jnp.int32, (16, LANES), 0)
    lane = lax.broadcasted_iota(jnp.int32, (16, LANES), 1)
    weights = jnp.zeros((16, LANES), jnp.float32)
    for side, taps in ((0, enumerate(EAST[15:21])), (8, enumerate(EAST[:5], LANES - 5))):
        for at, tap in taps:
            weights = jnp.where((row == side) & (lane == at), float(tap), weights)
    return weights


def edge_places():
    odd = lax.axis_index("gx") % 2
    row = lax.broadcasted_iota(jnp.int32, (ROWS, LANES), 0)
    lane = lax.broadcasted_iota(jnp.int32, (ROWS, LANES), 1)
    across = odd * (LANES - 1)
    return jnp.where((row == 0) & (lane == across) | (row == 1) & (lane == LANES - 1 - across), 1.0, 0.0)


def weighed(values, weight):
    scaled = [v * weight for v in values]
    return scaled + [scaled[a] * values[b] for a, b in PRODUCT_PAIRS]


def added(sums, terms):
    return [s + t for s, t in zip(sums, terms)]


def strided(tile, level, p):
    start = level * (tile.shape[1] // LEVELS) + p
    return [tile[c, pl.ds(start, ROWS, stride=RATIO), :] for c in range(COMPONENTS)]


def end_sums(tile, edge):
    height = tile.shape[1] // LEVELS
    row = lax.broadcasted_iota(jnp.int32, (ROWS, LANES), 0)
    total = None
    for p in range(6):
        ends = (pl.ds(p, LEVELS, stride=height), pl.ds(height - 6 + p, LEVELS, stride=height))
        values = [jnp.concatenate([tile[c, end, :] for end in ends], axis=0) for c in range(COMPONENTS)]
        terms = weighed(values, jnp.where(row < LEVELS, G[p + 15], G[p - 1] if p else 0.0))
        total = terms if total is None else added(total, terms)
    for q, value in enumerate(total):
        edge[pl.ds(q * ROWS, ROWS), :] = value


GROUPS = ((0, 1, 2, 3, 4, 5, 6, 7), (8, 9, 10, 11, 12, 13))


def filter_level(load, level, inner, edge=None):
    for group in GROUPS:

        def terms_of(p, weight):
            values = load(level, p)
            scaled = [v * weight for v in values]
            pairs = [PRODUCT_PAIRS[q - COMPONENTS] if q >= COMPONENTS else (q, None) for q in group]
            return [scaled[a] if b is None else scaled[a] * values[b] for a, b in pairs]

        own = below = terms_of(0, G[5])
        for p in range(1, 5):
            own = added(own, terms_of(p, G[p + 5]))
            below = added(below, terms_of(p, G[p + 15]))
        own = added(own, terms_of(5, G[10]))
        above = terms_of(5, G[0])
        below = added(below, above)
        if edge is not None:
            for q, value in zip(group, below):
                edge[pl.ds(q * ROWS + level, 1), :] = value[0:1]
        own = [o + pltpu.roll(v, ROWS - 1, 0) for o, v in zip(own, below)]
        for p in range(6, RATIO):
            own = added(own, terms_of(p, G[p + 5]))
            above = added(above, terms_of(p, G[p - 5]))
        for q, o, value in zip(group, own, above):
            inner[pl.ds((q * LEVELS + level) * ROWS, ROWS), :] = o + pltpu.roll(value, 1, 0)
            if edge is not None:
                edge[pl.ds(q * ROWS + LEVELS + level, 1), :] = value[ROWS - 1 : ROWS]


def tile_copies(fields, places, sems):
    return [
        pltpu.make_async_copy(fields.at[:, :, pl.ds(t * LANES, LANES)], place, sems.at[i])
        for i, (t, place) in enumerate(places)
    ]


def outer_kernel(order, fields, across, beside, ready, inner, edge, level_sems, sems):
    height = fields.shape[1] // LEVELS
    arriving = []
    for level in range(LEVELS):
        rows = pl.ds(level * height, height)
        arriving.append(
            [
                pltpu.make_async_copy(
                    fields.at[:, rows, pl.ds(order[i] * LANES, LANES)], ready.at[i, :, rows], level_sems.at[i, level]
                )
                for i in range(OUTER)
            ]
        )
    copies = tile_copies(fields, [(order[i], ready.at[i]) for i in range(OUTER, BROUGHT)], sems)
    for copy in sum(arriving, []) + copies:
        copy.start()
    lane = lax.broadcasted_iota(jnp.int32, (ROWS, LANES), 1)

    def merged(level, p):
        first, last = (strided(ready.at[i], level, p) for i in range(OUTER))
        return [jnp.where(lane < LANES // 2, f, s) for f, s in zip(first, last)]

    for level in range(LEVELS):
        for copy in arriving[level]:
            copy.wait()
        filter_level(merged, level, inner, edge)
    beyond = jnp.concatenate(split_here(beyond_weights()), axis=0)
    total = None
    for part in split_here(jnp.concatenate([inner[...], edge[...]], axis=0)):
        sums = lax.dot_general(beyond, part, (((1,), (1,)), ((), ())), preferred_element_type=jnp.float32)
        total = sums if total is None else total + sums
    messages = total[:16] + (total[16:32] + total[32:])
    odd = lax.axis_index("gx") % 2 == 1
    across[...] = jnp.where(odd, messages[8:9], messages[:1])
    beside[...] = jnp.where(odd, messages[:1], messages[8:9])
    for copy in copies:
        copy.wait()


def split_here(values):
    first = values.astype(jnp.bfloat16)
    left = values - first.astype(jnp.float32)
    second = left.astype(jnp.bfloat16)
    return first, second, (left - second.astype(jnp.float32)).astype(jnp.bfloat16)


def dot(a, b):
    return jnp.dot(a, b, preferred_element_type=jnp.float32)


def east_sums(values, pair, weights):
    rows = pl.ds(pair * 2 * LANES, 2 * LANES)
    a, b, c = split_here(values)
    both = dot(a, weights[rows, :]) + dot(b, weights[rows, :])
    return both[:, :LANES] + (both[:, LANES:] + dot(c, weights[rows, :LANES]))


def east_sums_stacked(values, pair, weights):
    parts = dot(jnp.concatenate(split_here(values), axis=0), weights[pl.ds(pair * 2 * LANES, 2 * LANES), :])
    count = values.shape[0]
    sums = parts[:count] + (parts[count : 2 * count] + parts[2 * count :])
    return sums[:, :LANES] + sums[:, LANES:]


def middle_kernel(order, fields, ready, weights, inner, partial, later, tile, edge, sems):
    places = [tile.at[i] for i in range(FULL - BROUGHT)] + [later.at[i] for i in range(len(order) - FULL)]
    copies = tile_copies(fields, list(zip(order[BROUGHT:], places)), sems)
    for copy in copies:
        copy.start()
    tiles = [ready.at[i] for i in range(BROUGHT)] + places

    def add(pair):
        both = jnp.concatenate([edge[2 * pair], edge[2 * pair + 1]], axis=1)
        part = east_sums_stacked(both, pair, weights)
        partial[...] = part if pair == 0 else partial[...] + part

    for i in range(len(order)):
        if i >= BROUGHT:
            copies[i - BROUGHT].wait()
        if i < FULL:
            for level in range(LEVELS):
                filter_level(functools.partial(strided, tiles[i]), level, inner.at[i], edge.at[i])
        else:
            end_sums(tiles[i], edge.at[i])
    for pair in range(len(order) // 2):
        add(pair)


def from_sides(across, beside):
    none = jnp.zeros((ROWS - 2, across.shape[1]), jnp.float32)
    both = jnp.concatenate([across, beside, none], axis=0)
    return lax.dot_general(
        both, edge_places(), (((0,), (0,)), ((), ())), precision=HIGHEST, preferred_element_type=jnp.float32
    )


def corner_kernel(partial, across, beside, before, after):
    start = TERMS * LEVELS * ROWS
    total = partial[...] + from_sides(across[:, start:], beside[:, start:])
    for q in range(TERMS):
        rows = pl.ds(q * LEVELS, LEVELS)
        before[rows, :] = total[q * ROWS : q * ROWS + LEVELS]
        after[rows, :] = total[q * ROWS + LEVELS : (q + 1) * ROWS]


def coarse_kernel(full_inner, later, weights, across, beside, coarse, inner):
    count = later.shape[0]
    tiles = [full_inner.at[i] for i in range(FULL)] + [inner.at[i] for i in range(count)]
    stop = TERMS * LEVELS * ROWS
    coarse[...] = from_sides(across[:, :stop], beside[:, :stop])

    def add(pair):
        both = jnp.concatenate([tiles[2 * pair][...], tiles[2 * pair + 1][...]], axis=1)
        coarse[...] += east_sums(both, pair, weights)

    done = 0
    for i in range(count):
        if 2 * done + 2 <= FULL + i:
            add(done)
            done += 1
        for level in range(LEVELS):
            filter_level(functools.partial(strided, later.at[i]), level, inner.at[i])
    for pair in range(done, len(tiles) // 2):
        add(pair)


def send_kernel(cap, coarse, south, north, before, after, owner, outgoing, filtered, spread):
    filtered[...] = coarse[...]
    slab = LEVELS * ROWS
    filtered[pl.ds(0, EDGE, stride=ROWS), :] += south[...] - after[...]
    filtered[pl.ds(ROWS - 1, EDGE, stride=ROWS), :] += north[...] - before[...]
    means = [filtered[c * slab : (c + 1) * slab, :] for c in range(COMPONENTS)]
    lane = lax.broadcasted_iota(jnp.int32, (slab, LANES), 1) % BLK
    for k, (a, b) in enumerate(PRODUCT_PAIRS):
        q = COMPONENTS + k
        stress = filtered[q * slab : (q + 1) * slab, :] - means[a] * means[b]
        for c in range(BLK):
            spread[pl.ds(k * slab * BLK + c, slab, stride=BLK), :] = jnp.where(lane == c, stress, 0.0)
    slots = outgoing.shape[0] * outgoing.shape[1]
    blocks = owner.shape[1]
    across = LANES // BLK
    own = lax.broadcasted_iota(jnp.int32, (blocks, blocks), 0) == lax.broadcasted_iota(jnp.int32, (blocks, blocks), 1)
    column = jnp.sum(jnp.where(own, jnp.broadcast_to(owner[...], (blocks, blocks)), 0), axis=1, keepdims=True)
    index = lax.broadcasted_iota(jnp.int32, (blocks, LANES), 0)
    named = jnp.broadcast_to(column, (blocks, LANES))
    slot_row = lax.broadcasted_iota(jnp.int32, (slots, LANES), 0)
    stresses = spread[...].reshape(len(PRODUCT_PAIRS) * LEVELS, blocks // across, BLK * BLK, LANES)
    picks, payloads = [], []
    for by in range(blocks // across):
        block = by * across + lax.broadcasted_iota(jnp.int32, (blocks, LANES), 1) // BLK
        mine = jnp.sum(jnp.where(index == block, named, 0), axis=0, keepdims=True)
        earlier = jnp.where((index < block) & (named == mine), 1, 0)
        slot = mine * cap + jnp.sum(earlier, axis=0, keepdims=True)
        picks.append(jnp.where(slot_row == slot, 1.0, 0.0).astype(jnp.bfloat16))
        payloads.append(stresses[:, by].reshape(-1, LANES))
    chosen = jnp.concatenate(picks, axis=1)
    total = None
    for part in split_here(jnp.concatenate(payloads, axis=1)):
        sums = lax.dot_general(chosen, part, (((1,), (1,)), ((), ())), preferred_element_type=jnp.float32)
        total = sums if total is None else total + sums
    for d in range(outgoing.shape[0]):
        outgoing[d] = total[d * cap : (d + 1) * cap]


def place_kernel(arrived, received, rows, sems):
    parts = rows.shape[0]
    sources, cap, _ = arrived.shape
    count = sources // parts
    copies = []
    for part in range(parts):
        for d in range(count):
            rows[part, pl.ds(d * cap, cap), :] = arrived[part * count + d]
        copies.append(
            pltpu.make_async_copy(
                rows.at[part], received.at[pl.ds(part * count * cap, count * cap), :], sems.at[part]
            )
        )
        copies[-1].start()
    for copy in copies:
        copy.wait()


def call(kernel, out_shape, *args, scratch=(), hbm=0, out=pltpu.VMEM):
    whole = pl.BlockSpec(memory_space=pltpu.VMEM)
    held = [pltpu.with_memory_space_constraint(a, pltpu.VMEM if i >= hbm else pltpu.HBM) for i, a in enumerate(args)]
    return pl.pallas_call(
        kernel,
        out_shape=out_shape,
        in_specs=[pl.BlockSpec(memory_space=pltpu.HBM)] * hbm + [whole] * (len(args) - hbm),
        out_specs=jax.tree.map(lambda _: pl.BlockSpec(memory_space=out), out_shape),
        scratch_shapes=list(scratch),
        compiler_params=pltpu.CompilerParams(vmem_limit_bytes=VMEM_BYTES),
    )(*held)


def f32(*shape):
    return jax.ShapeDtypeStruct(shape, jnp.float32)


def per_device(fields, owner):
    _, _, height, width = fields.shape
    tiles = width // LANES
    rows = TERMS * LEVELS * ROWS
    flat = fields.reshape(COMPONENTS, LEVELS * height, width)
    lane_tile = (COMPONENTS, LEVELS * height, LANES)
    order = (0, tiles - 1) + tuple(range(1, tiles - 1))
    weights = jnp.asarray(split_weights(width, order))
    rest = tiles - FULL
    message = f32(1, rows + 2 * EDGE)
    to_across, to_beside, ready = call(
        functools.partial(outer_kernel, order),
        (message, message, f32(BROUGHT, *lane_tile)),
        flat,
        scratch=[
            pltpu.VMEM((rows, LANES), jnp.float32),
            pltpu.VMEM((2 * EDGE, LANES), jnp.float32),
            pltpu.SemaphoreType.DMA((OUTER, LEVELS)),
            pltpu.SemaphoreType.DMA((BROUGHT - OUTER,)),
        ],
        hbm=1,
    )
    nx, ny = lax.axis_size("gx"), lax.axis_size("gy")
    beside_x = [(i, i ^ 1) for i in range(nx)]
    across_x = [(i, (i + 1) % nx if i % 2 else (i - 1) % nx) for i in range(nx)]
    up_y = [(i, (i + 1) % ny) for i in range(ny)]
    down_y = [(j, i) for i, j in up_y]
    across = lax.ppermute(to_across, "gx", across_x)
    beside = lax.ppermute(to_beside, "gx", beside_x)
    full_inner, partial, later = call(
        functools.partial(middle_kernel, order),
        (f32(FULL, rows, LANES), f32(2 * EDGE, LANES), f32(rest, *lane_tile)),
        flat,
        ready,
        weights,
        scratch=[
            pltpu.VMEM((FULL - BROUGHT, *lane_tile), jnp.float32),
            pltpu.VMEM((tiles, 2 * EDGE, LANES), jnp.float32),
            pltpu.SemaphoreType.DMA((tiles - BROUGHT,)),
        ],
        hbm=1,
    )
    before, after = call(corner_kernel, (f32(EDGE, LANES), f32(EDGE, LANES)), partial, across, beside)
    from_south = lax.ppermute(after, "gy", up_y)
    from_north = lax.ppermute(before, "gy", down_y)
    coarse = call(
        coarse_kernel,
        f32(rows, LANES),
        full_inner,
        later,
        weights,
        across,
        beside,
        scratch=[pltpu.VMEM((rest, rows, LANES), jnp.float32)],
    )
    devices = nx * ny
    blocks = owner.shape[0]
    cap = max(2, 2 * blocks // devices)
    pay = len(PRODUCT_PAIRS) * LEVELS * BLK * BLK
    outgoing = call(
        functools.partial(send_kernel, cap),
        f32(devices, cap, pay),
        coarse,
        from_south,
        from_north,
        before,
        after,
        owner.reshape(1, blocks),
        scratch=[pltpu.VMEM((rows, LANES), jnp.float32), pltpu.VMEM((pay * blocks * BLK // LANES, LANES), jnp.float32)],
    )
    arrived = lax.all_to_all(outgoing, ("gx", "gy"), split_axis=0, concat_axis=0, tiled=True)
    parts = 4
    return call(
        place_kernel,
        f32(devices * cap, pay),
        arrived,
        scratch=[pltpu.VMEM((parts, devices * cap // parts, pay), jnp.float32), pltpu.SemaphoreType.DMA((parts,))],
        out=pltpu.HBM,
    )


def solution(mesh):
    placed = (P(None, None, "gy", "gx"), P(("gx", "gy"), None))
    return jax.shard_map(
        per_device, mesh=mesh, in_specs=placed, out_specs=P(("gx", "gy"), None), check_vma=False
    )
```
